512 devices in a mesh: row: 64 (over x, z, core), col: 8 (over y).
Axes of the slice: x: 4, y: 8, z: 8, core: 2. Of those that a mesh axis runs over, the one named last changes fastest.
Arguments:
- right_side: bfloat16 [31, 2048, 256], P(None, ('row', 'col')), may hold values from -6 to 6
- lower_blocks: bfloat16 [98, 2048, 2048], P(None, 'row', 'col'), may hold values from -0.0625 to 0.0625
- upper_blocks: bfloat16 [98, 2048, 2048], P(None, 'row', 'col'), may hold values from -0.0625 to 0.0625
- pivot_inverse: bfloat16 [31, 2048, 2048], P(None, 'row', 'col'), may hold values from -0.125 to 0.125
- widths: int32 [31], replicated, may hold values from 512 to 2048, as said below
- first_row: int32 [31, 4], replicated, may hold values from 0 to 1024, as said below
Outputs:
- solution: bfloat16 [31, 2048, 256], P(None, ('row', 'col'))
The draws below stay inside these ranges and needn't reach their ends.
Inputs may be any that keep to these rules, and one draw needn't show every extreme that they name: Rows at or past widths[n] of supernode n are outside the supernode: right_side may hold any values there, and valid sets y and solution to zero in them. `first_row`: entry k of node n is used only for k below the depth of n.
All inputs are finite; a program needn't handle non-finite values.
Results may differ from the reference program's by a relative error of at most 0.008.
Values may be sent and summed in bfloat16 or wider, within the bound.
A program may use at most 64 MiB of HBM per device.

```python
import jax
import jax.numpy as jnp

LEVELS = 5
SN = 2048
NRHS = 256
NODES = 31
NBLK = 98
PROC_ROWS = 64
PROC_COLS = 8
CYC = 4


def draw_widths(key, part):
    key = jax.random.fold_in(key, 11)
    first_key, second_key = jax.random.split(key)
    values = jax.random.randint(first_key, (NODES,), SN // 4, SN + 1, dtype=jnp.int32)
    chosen = jax.random.permutation(second_key, NODES)[:2]
    values = values.at[chosen[0]].set(SN).at[chosen[1]].set(SN // 4)
    return values


def draw_first_row(key, part):
    key = jax.random.fold_in(key, 23)
    first_key, second_key = jax.random.split(key)
    entries = NODES * (LEVELS - 1)
    values = jax.random.randint(first_key, (entries,), 0, SN // 2 + 1, dtype=jnp.int32)
    chosen = jax.random.permutation(second_key, entries)[:2]
    values = values.at[chosen[0]].set(SN // 2).at[chosen[1]].set(0)
    return values.reshape(NODES, LEVELS - 1)


def steps_of(key, extent, cuts, least, top_value):
    level = 1.0
    for dim, blocks in cuts:
        draws = jax.random.uniform(jax.random.fold_in(jax.random.fold_in(key, 6), dim), (blocks,), jnp.float32, least / len(cuts), top_value / len(cuts))
        level = level * jnp.repeat(jnp.exp(draws), extent[dim] // blocks).reshape((-1,) + (1,) * (len(extent) - 1 - dim))
    return level


def gaussian(stream_key, dims, scale, bound, cuts=(), kind=jnp.bfloat16):
    drawn = scale * jax.random.normal(stream_key, dims, jnp.float32)
    if cuts:
        drawn = drawn * steps_of(stream_key, dims, cuts, -0.22, 0.18)
    return jnp.clip(drawn, -bound, bound).astype(kind)


def setup_inputs(seed: int = 0) -> dict:
    streams_of = jax.random.split(jax.random.key(seed), 7)
    return {
        "right_side": gaussian(streams_of[0], (NODES, SN, NRHS), 1.0, 6.0, ((1, 512),)),
        "lower_blocks": gaussian(streams_of[1], (NBLK, SN, SN), (4 * SN) ** -0.5, 0.0625, ((1, 64), (2, 8))),
        "upper_blocks": gaussian(streams_of[2], (NBLK, SN, SN), (4 * SN) ** -0.5, 0.0625, ((1, 64), (2, 8))),
        "pivot_inverse": gaussian(streams_of[3], (NODES, SN, SN), SN ** -0.5, 0.125, ((1, 64), (2, 8))),
        "widths": draw_widths(jax.random.fold_in(streams_of[6], 71), 0),
        "first_row": draw_first_row(jax.random.fold_in(streams_of[6], 71), 0),
    }


def block_offsets():
    offsets = {}
    running = 0
    for tree_level in range(1, LEVELS):
        for hop_up in range(tree_level):
            offsets[(tree_level, hop_up)] = running
            running = running + 2 ** tree_level
    return offsets


def stored_order(vectors):
    node_count = vectors.shape[0]
    columns = vectors.shape[2]
    shaped = vectors.reshape(node_count, PROC_ROWS, PROC_COLS, CYC, columns)
    return jnp.transpose(shaped, (0, 2, 1, 3, 4)).reshape(node_count, SN, columns)


def apply_blocks(blocks, vectors):
    return jnp.einsum("nij,njr->nir", blocks.astype(jnp.float32), stored_order(vectors).astype(jnp.float32))


def reference(right_side, lower_blocks, upper_blocks, pivot_inverse, widths, first_row):
    offsets = block_offsets()
    row_index = jnp.arange(SN, dtype=jnp.int32)
    valid_rows = (row_index[None, :] < widths[:, None]).astype(jnp.float32)[:, :, None]
    couple = (row_index[None, None, :] >= first_row[:, :, None]).astype(jnp.float32)
    pending = [jnp.zeros((2 ** tree_level, SN, NRHS), jnp.float32) for tree_level in range(LEVELS)]
    forward = [None] * LEVELS
    for tree_level in range(LEVELS - 1, -1, -1):
        first_node = 2 ** tree_level - 1
        span_nodes = 2 ** tree_level
        source = right_side[first_node:first_node + span_nodes].astype(jnp.float32) - pending[tree_level]
        solved = (valid_rows[first_node:first_node + span_nodes] * source).astype(jnp.bfloat16)
        forward[tree_level] = solved
        for hop_up in range(tree_level):
            block_start = offsets[(tree_level, hop_up)]
            product = apply_blocks(lower_blocks[block_start:block_start + span_nodes], solved)
            product = product * couple[first_node:first_node + span_nodes, hop_up][:, :, None]
            target = tree_level - 1 - hop_up
            grouped = product.reshape(2 ** target, 2 ** (hop_up + 1), SN, NRHS).sum(axis=1)
            pending[target] = pending[target] + grouped
    scaled = apply_blocks(pivot_inverse, jnp.concatenate(forward, axis=0))
    behind = [jnp.zeros((2 ** tree_level, SN, NRHS), jnp.float32) for tree_level in range(LEVELS)]
    answer = []
    for tree_level in range(LEVELS):
        first_node = 2 ** tree_level - 1
        span_nodes = 2 ** tree_level
        source = scaled[first_node:first_node + span_nodes] - behind[tree_level]
        solved = (valid_rows[first_node:first_node + span_nodes] * source).astype(jnp.bfloat16)
        answer.append(solved)
        for lower_level in range(tree_level + 1, LEVELS):
            hop_up = lower_level - 1 - tree_level
            lower_first = 2 ** lower_level - 1
            lower_span = 2 ** lower_level
            repeated = jnp.repeat(solved, 2 ** (hop_up + 1), axis=0).astype(jnp.float32)
            masked = repeated * couple[lower_first:lower_first + lower_span, hop_up][:, :, None]
            block_start = offsets[(lower_level, hop_up)]
            behind[lower_level] = behind[lower_level] + apply_blocks(upper_blocks[block_start:block_start + lower_span], masked)
    return jnp.concatenate(answer, axis=0)
```

```python
import functools

import jax
import jax.numpy as jnp
from jax import lax
from jax.experimental import pallas as pl
from jax.experimental.pallas import tpu as pltpu
from jax.sharding import PartitionSpec as P

MESH = pl.DeviceIdType.MESH
BF = jnp.bfloat16
F32 = jnp.float32
LEVELS = 5
NX, NZ, NC = 4, 8, 8
NQ = NX * NZ
GROUPS = [1, 1, 1, 2, 4]
GBASE = [8, 7, 6, 4, 0]
NGROUP = 9
GROUP = 16


def block_offsets():
    offsets = {}
    running = 0
    for tree_level in range(1, LEVELS):
        for hop_up in range(tree_level):
            offsets[tree_level, hop_up] = running
            running = running + 2**tree_level
    return offsets


OFF = block_offsets()


def forward_rows(t):
    rows, at = [], 0
    for hop in range(t):
        count = 32 * (2 if hop == 0 and t >= 2 else 1)
        rows.append((t - 1 - hop, at, count))
        at += count
    count = 32 * min(4, 2**t)
    rows.append((-1, at, count))
    return rows, at + count


def backward_rows(t):
    rows, at = [], 0
    for s in range(t + 1, LEVELS):
        count = 32 * min(4, 2**t) * 2 ** (s - t)
        rows.append((s, at, count))
        at += count
    return rows, at


FROWS = [forward_rows(t) for t in range(LEVELS)]
BROWS = [backward_rows(t) for t in range(LEVELS - 1)]


def kernel(rs_ref, widths_ref, first_ref, l_hbm, u_hbm, d_hbm, out_ref, scratch):
    row = lax.axis_index("row")
    col = lax.axis_index("col")
    x, z, core = row // 16, (row // 2) % 8, row % 2
    q = x * NZ + z
    other = 1 - core
    lw, uw, dw, sel, perm = (scratch[n] for n in ("lw", "uw", "dw", "sel", "perm"))
    fw, bw, pend, acc = (scratch[n] for n in ("fw", "bw", "pend", "acc"))
    gather, relay_sem, load_sem = scratch["gather"], scratch["relay_sem"], scratch["load_sem"]
    slabs, sums, ring_sem = scratch["slabs"], scratch["sums"], scratch["ring_sem"]

    loads = [
        pltpu.make_async_copy(src, dst, load_sem.at[i])
        for i, (src, dst) in enumerate(((l_hbm, lw), (u_hbm, uw), (d_hbm, dw)))
    ]
    for load in loads:
        load.start()

    barrier = pltpu.get_barrier_semaphore()

    def plane_peer(k):
        px, pz = (x + k // NZ) % NX, (z + k % NZ) % NZ
        return (px * NZ + pz) * 2 + core

    def signal(target):
        pl.semaphore_signal(barrier, inc=1, device_id=target, device_id_type=MESH)

    @pl.loop(1, NQ)
    def _(k):
        signal({"row": plane_peer(k)})

    @pl.loop(1, NC)
    def _(k):
        signal({"col": (col + k) % NC})

    signal({"row": q * 2 + other})

    row16 = lax.broadcasted_iota(jnp.int32, (GROUP, 256), 0)
    own_row = row * 32 + col * 4 + row16 % 4

    def valid(t, g):
        limit = jnp.zeros((GROUP, 256), jnp.int32)
        for j in range(min(4, 2**t)):
            limit = jnp.where(row16 // 4 == j, widths_ref[2**t - 1 + 4 * g + j], limit)
        return (own_row < limit).astype(F32)

    def piece(t, g):
        at = (GBASE[t] + g) * GROUP
        return slice(at, at + GROUP)

    for g in range(4):
        y = valid(4, g) * rs_ref[piece(4, g)].astype(F32)
        gather["f4"][g, core, q] = y.astype(BF)

    @pl.loop(0, 2)
    def _(h):
        @pl.loop(0, 8)
        def _(b):
            r = lax.broadcasted_iota(jnp.int32, (128, 512), 0) + b * 128
            s = lax.broadcasted_iota(jnp.int32, (128, 512), 1)
            p = (r % 256) // 4
            target = (p // 2) * 16 + (r // 256) * 4 + r % 4
            hit = jnp.logical_and(s == target, p % 2 == h)
            sel[h, pl.ds(pl.multiple_of(b * 128, 128), 128)] = hit.astype(F32).astype(BF)

    r = lax.broadcasted_iota(jnp.int32, (128, 128), 0)
    s = lax.broadcasted_iota(jnp.int32, (128, 128), 1)
    perm[...] = (s == ((r // 4) % 4) * 32 + (r // 16) * 4 + r % 4).astype(F32).astype(BF)
    for t in range(LEVELS - 1):
        pend[t][...] = jnp.zeros_like(pend[t])

    out_row = row * 32 + lax.broadcasted_iota(jnp.int32, (32, 256), 0)
    lane = lax.broadcasted_iota(jnp.int32, (32, 256), 1)
    in_row = (lane // 4) * 32 + col * 4 + lane % 4

    def mask(ref, index, t, hop):
        @pl.loop(0, 2**t)
        def _(n):
            keep = (index >= first_ref[2**t - 1 + n, hop]).astype(F32).astype(BF)
            ref[OFF[t, hop] + n] = ref[OFF[t, hop] + n] * keep

    def stack(ref, base, groups, members):
        return jnp.concatenate(
            [
                jnp.concatenate([ref[base + 4 * g + j] for j in members], axis=1)
                for g in range(groups)
            ],
            axis=0,
        )

    def expand_forward(t):
        groups = GROUPS[t]
        for target, at, count in FROWS[t][0]:
            if target >= 0:
                hop = t - 1 - target
                halves = count // 32
                per = min(4, 2**t) // halves
                jobs = [
                    (lw, OFF[t, hop], at + 32 * v, [v * per + w for w in range(per)])
                    for v in range(halves)
                ]
            else:
                jobs = [(dw, 2**t - 1, at + 32 * j, [j]) for j in range(count // 32)]
            for ref, base, first, members in jobs:
                left = stack(ref, base, groups, members)

                @pl.loop(0, 2)
                def _(h):
                    table = sel[h, members[0] * 256 : (members[-1] + 1) * 256]
                    wide = jnp.dot(left, table, preferred_element_type=F32).astype(BF)
                    for g in range(groups):
                        fw[t][g, h, first : first + 32] = wide[g * 32 : (g + 1) * 32]

    def expand_backward(t):
        for g in range(GROUPS[t]):
            for s, at, count in BROWS[t][0]:
                each = 2 ** (s - t)
                for j in range(min(4, 2**t)):
                    base = OFF[s, s - 1 - t] + (4 * g + j) * each
                    left = uw[base : base + each].reshape(each * 32, 256)
                    first = at + j * each * 32

                    @pl.loop(0, 2)
                    def _(h):
                        table = sel[h, j * 256 : (j + 1) * 256]
                        wide = jnp.dot(left, table, preferred_element_type=F32).astype(BF)
                        bw[t][g, h, first : first + each * 32] = wide

    def remote(src, dst, number, target):
        return pltpu.make_async_remote_copy(
            src_ref=src,
            dst_ref=dst,
            send_sem=relay_sem.at[0, number],
            recv_sem=relay_sem.at[1, number],
            device_id=target,
            device_id_type=MESH,
        )

    def spread(name, number):
        ref = gather[name]

        @pl.loop(1, NQ)
        def _(k):
            mine = ref.at[core, q]
            remote(mine, mine, number, {"row": plane_peer(k)}).start()

    def spread_wait(name, number):
        some = gather[name].at[core, 0 : NQ - 1]
        remote(some, some, number, {"row": q * 2 + other}).wait_recv()

    def share(ref, number):
        half = ref.at[core]
        remote(half, half, number, {"row": q * 2 + other}).start()

    def share_wait(ref, number):
        half = ref.at[other]
        remote(half, half, number, {"row": q * 2 + other}).wait_recv()

    def ring(src, dst, number, target):
        return pltpu.make_async_remote_copy(
            src_ref=src,
            dst_ref=dst,
            send_sem=ring_sem.at[0, number],
            recv_sem=ring_sem.at[1, number],
            device_id={"col": target},
            device_id_type=MESH,
        )

    def reduce_start(source, t, number):
        slab, landing = slabs[number], sums[number]
        have = min(4, 2**t) * 32
        for g in range(GROUPS[t]):
            part = source[g * 128 : g * 128 + have].astype(BF)
            cut = jnp.dot(perm[:, :have], part, preferred_element_type=F32).astype(BF)
            slab[:, g * GROUP : (g + 1) * GROUP] = cut.reshape(NC, GROUP, 256)

        @pl.loop(1, NC)
        def _(k):
            to = (col + k) % NC
            ring(slab.at[to], landing.at[col], number, to).start()

        landing[col] = slab[col]

    def reduce_wait(number):
        some = sums[number].at[0 : NC - 1]
        ring(some, some, number, (col + 1) % NC).wait_recv()

    def reduced(number, g):
        landing = sums[number]
        at = slice(g * GROUP, (g + 1) * GROUP)
        total = landing[0, at].astype(F32)
        for k in range(1, NC):
            total = total + landing[k, at].astype(F32)
        return total

    def product(weights, ref, g, h, first, count, lead=None):
        at = ref.shape[2] // GROUP
        block = ref[h] if at == 1 else ref[h, :, g * GROUP : (g + 1) * GROUP]
        wg = g if weights.shape[0] > 1 else 0
        return jnp.dot(
            weights[wg, h, first : first + count],
            block.reshape(NQ * GROUP, 256),
            preferred_element_type=F32,
        )

    def add_forward(t, g, h, ref, block, entry, start):
        target, at, count = entry
        weights = fw[t][g, h, at : at + count]
        value = jnp.dot(weights, block(ref, h), preferred_element_type=F32)
        if target < 0:
            base = g * 128
            if start:
                acc[t][base : base + count] = value
            else:
                acc[t][base : base + count] += value
        else:
            first = ((4 * g) >> (t - target)) * 32
            pend[target][first : first + count] += value

    def add_backward(t, g, h, ref, block, entry):
        s, at, count = entry
        weights = bw[t][g, h, at : at + count]
        value = jnp.dot(weights, block(ref, h), preferred_element_type=F32)
        first = g * 128 * 2 ** (s - t)
        acc[s][first : first + count] -= value

    def block_of(g):
        def block(ref, h):
            return ref[h, :, g * GROUP : (g + 1) * GROUP].reshape(NQ * GROUP, 256)

        return block

    def block_all(ref, h):
        return ref[h].reshape(NQ * GROUP, 256)

    for load in loads[:1]:
        load.wait()
    for t in range(4, 0, -1):
        for hop in range(t):
            mask(lw, out_row, t, hop)
    loads[2].wait()
    expand_forward(4)
    pl.semaphore_wait(barrier, NQ - 1 + NC - 1 + 1)

    f4 = gather["f4"]
    for g in range(4):

        @pl.loop(1, NZ)
        def _(k):
            mine = f4.at[g, core, q]
            remote(mine, mine, 3 * g, {"row": (x * NZ + (z + k) % NZ) * 2 + core}).start()

    expand_forward(3)
    expand_forward(2)
    for g in range(4):
        some = f4.at[g, core, 0 : NZ - 1]
        remote(some, some, 3 * g, {"row": q * 2 + other}).wait_recv()

        @pl.loop(1, NX)
        def _(k):
            line = f4.at[g, core, pl.ds(x * NZ, NZ)]
            remote(line, line, 3 * g + 1, {"row": (((x + k) % NX) * NZ + z) * 2 + core}).start()

    expand_forward(1)
    expand_forward(0)
    for g in range(4):
        some = f4.at[g, core, 0 : NQ - NZ]
        remote(some, some, 3 * g + 1, {"row": q * 2 + other}).wait_recv()
        share(f4.at[g], 3 * g + 2)
        add_forward(4, g, core, f4.at[g], block_all, FROWS[4][0][0], True)
        if g > 0:
            share_wait(f4.at[g - 1], 3 * (g - 1) + 2)
            add_forward(4, g - 1, other, f4.at[g - 1], block_all, FROWS[4][0][0], False)
    share_wait(f4.at[3], 11)
    add_forward(4, 3, other, f4.at[3], block_all, FROWS[4][0][0], False)
    reduce_start(pend[3], 3, 0)
    for g in range(4):
        for entry in FROWS[4][0][1:]:
            add_forward(4, g, core, f4.at[g], block_all, entry, True)
            add_forward(4, g, other, f4.at[g], block_all, entry, False)
    loads[1].wait()

    number = 12
    for t in range(3, -1, -1):
        name = f"f{t}"
        ref = gather[name]
        reduce_wait(3 - t)
        for g in range(GROUPS[t]):
            y = rs_ref[piece(t, g)].astype(F32) - reduced(3 - t, g)
            ref[core, q, g * GROUP : (g + 1) * GROUP] = (valid(t, g) * y).astype(BF)
        spread(name, number)
        if t == 3:
            for s in range(1, LEVELS):
                for hop in range(s):
                    mask(uw, in_row, s, hop)
            expand_backward(0)
        else:
            expand_backward(3 - t)
        spread_wait(name, number)
        share(ref, number + 1)
        for g in range(GROUPS[t]):
            add_forward(t, g, core, ref, block_of(g), FROWS[t][0][0], True)
        share_wait(ref, number + 1)
        for g in range(GROUPS[t]):
            add_forward(t, g, other, ref, block_of(g), FROWS[t][0][0], False)
        if t > 0:
            reduce_start(pend[t - 1], t - 1, 4 - t)
            for g in range(GROUPS[t]):
                for entry in FROWS[t][0][1:]:
                    add_forward(t, g, core, ref, block_of(g), entry, True)
                    add_forward(t, g, other, ref, block_of(g), entry, False)
        else:
            reduce_start(acc[0], 0, 4)
        number += 2

    for t in range(LEVELS):
        name = f"b{t}"
        reduce_wait(4 + t)
        for g in range(GROUPS[t]):
            solved = (valid(t, g) * reduced(4 + t, g)).astype(BF)
            out_ref[piece(t, g)] = solved
            if t < 4:
                gather[name][core, q, g * GROUP : (g + 1) * GROUP] = solved
        if t == 4:
            break
        ref = gather[name]
        spread(name, number)
        spread_wait(name, number)
        share(ref, number + 1)
        for g in range(GROUPS[t]):
            add_backward(t, g, core, ref, block_of(g), BROWS[t][0][0])
        share_wait(ref, number + 1)
        for g in range(GROUPS[t]):
            add_backward(t, g, other, ref, block_of(g), BROWS[t][0][0])
        reduce_start(acc[t + 1], t + 1, 5 + t)
        for g in range(GROUPS[t]):
            for entry in BROWS[t][0][1:]:
                add_backward(t, g, core, ref, block_of(g), entry)
                add_backward(t, g, other, ref, block_of(g), entry)
        number += 2

    for g in range(4):
        sent = f4.at[g, core, 0 : NZ - 1]
        remote(sent, sent, 3 * g, {"row": q * 2 + other}).wait_send()
        sent = f4.at[g, core, 0 : NQ - NZ]
        remote(sent, sent, 3 * g + 1, {"row": q * 2 + other}).wait_send()
        sent = f4.at[g, core]
        remote(sent, sent, 3 * g + 2, {"row": q * 2 + other}).wait_send()
    number = 12
    for name in ("f3", "f2", "f1", "f0", "b0", "b1", "b2", "b3"):
        sent = gather[name].at[core, 0 : NQ - 1]
        remote(sent, sent, number, {"row": q * 2 + other}).wait_send()
        sent = gather[name].at[core]
        remote(sent, sent, number + 1, {"row": q * 2 + other}).wait_send()
        number += 2
    for i in range(9):
        sent = sums[i].at[0 : NC - 1]
        ring(sent, sent, i, (col + 1) % NC).wait_send()


def scratch_shapes():
    gather = {"f4": pltpu.VMEM((4, 2, NQ, GROUP, 256), BF)}
    for t in range(4):
        for way in "fb":
            gather[f"{way}{t}"] = pltpu.VMEM((2, NQ, GROUP * GROUPS[t], 256), BF)
    order = [3, 2, 1, 0, 0, 1, 2, 3, 4]
    return {
        "lw": pltpu.VMEM((98, 32, 256), BF),
        "uw": pltpu.VMEM((98, 32, 256), BF),
        "dw": pltpu.VMEM((31, 32, 256), BF),
        "sel": pltpu.VMEM((2, 1024, 512), BF),
        "perm": pltpu.VMEM((128, 128), BF),
        "fw": [pltpu.VMEM((GROUPS[t], 2, FROWS[t][1], 512), BF) for t in range(5)],
        "bw": [pltpu.VMEM((GROUPS[t], 2, BROWS[t][1], 512), BF) for t in range(4)],
        "pend": [pltpu.VMEM((32 * 2**t, 256), F32) for t in range(4)],
        "acc": [pltpu.VMEM((32 * 2**t, 256), F32) for t in range(5)],
        "gather": gather,
        "slabs": [pltpu.VMEM((NC, GROUP * GROUPS[t], 256), BF) for t in order],
        "sums": [pltpu.VMEM((NC, GROUP * GROUPS[t], 256), BF) for t in order],
        "relay_sem": pltpu.SemaphoreType.DMA((2, 28)),
        "ring_sem": pltpu.SemaphoreType.DMA((2, 9)),
        "load_sem": pltpu.SemaphoreType.DMA((3,)),
    }


def shards(right_side, lower_blocks, upper_blocks, pivot_inverse, widths, first_row):
    zero = jnp.zeros((3, 4, 256), BF)
    padded = jnp.concatenate(
        [
            right_side[15:31],
            right_side[7:15],
            right_side[3:7],
            right_side[1:3],
            zero[:2],
            right_side[0:1],
            zero,
        ],
        axis=0,
    ).reshape(NGROUP * GROUP, 256)
    vmem = pl.BlockSpec(memory_space=pltpu.VMEM)
    smem = pl.BlockSpec(memory_space=pltpu.SMEM)
    hbm = pl.BlockSpec(memory_space=pl.ANY)
    shapes = scratch_shapes()
    leaves, tree = jax.tree.flatten(shapes)

    def body(*refs):
        kernel(*refs[:7], jax.tree.unflatten(tree, refs[7:]))

    answer = pl.pallas_call(
        body,
        out_shape=jax.ShapeDtypeStruct((NGROUP * GROUP, 256), BF),
        in_specs=[vmem, smem, smem, hbm, hbm, hbm],
        out_specs=vmem,
        scratch_shapes=leaves,
        compiler_params=pltpu.CompilerParams(
            collective_id=1, has_side_effects=True, vmem_limit_bytes=56 * 1024 * 1024
        ),
        name="tree_solve",
    )(padded, widths, first_row, lower_blocks, upper_blocks, pivot_inverse)
    nodes = answer.reshape(NGROUP * 4, 4, 256)
    return jnp.concatenate(
        [nodes[32:33], nodes[28:30], nodes[24:28], nodes[16:24], nodes[0:16]], axis=0
    )


def solution(mesh):
    in_specs = (
        P(None, ("row", "col"), None),
        P(None, "row", "col"),
        P(None, "row", "col"),
        P(None, "row", "col"),
        P(),
        P(),
    )
    out_specs = P(None, ("row", "col"), None)
    return jax.shard_map(shards, mesh=mesh, in_specs=in_specs, out_specs=out_specs, check_vma=False)
```

```python
import functools

import jax
import jax.numpy as jnp
from jax import lax
from jax.experimental import pallas as pl
from jax.experimental.pallas import tpu as pltpu
from jax.sharding import PartitionSpec as P

MESH = pl.DeviceIdType.MESH
BF = jnp.bfloat16
F32 = jnp.float32
LEVELS = 5
NX, NZ, NC = 4, 8, 8
NQ = NX * NZ
TOP = 2
GROUPS = [1, 1, 1, 2, 4]
GBASE = [7, 7, 6, 4, 0]
NGROUP = 8
GROUP = 16


def block_offsets():
    offsets = {}
    running = 0
    for tree_level in range(1, LEVELS):
        for hop_up in range(tree_level):
            offsets[tree_level, hop_up] = running
            running = running + 2**tree_level
    return offsets


OFF = block_offsets()


def forward_rows(t):
    rows, at = [], 0
    for hop in range(t):
        count = 64 if hop == 0 else 32
        rows.append((t - 1 - hop, at, count))
        at += count
    rows.append((-1, at, 128))
    return rows, at + 128


def backward_rows(t):
    rows, at = [], 0
    for s in range(t + 1, LEVELS):
        count = 32 * (2**s if t == 1 else 4 * 2 ** (s - t))
        rows.append((s, at, count))
        at += count
    return rows, at


FROWS = {t: forward_rows(t) for t in range(TOP, LEVELS)}
BROWS = {t: backward_rows(t) for t in range(1, LEVELS - 1)}
TL, TU, TD, TOPS = 0, 2, 4, 7
R3, R2, P1, P0, SPLIT, B2, B3, B4, PANEL, MPANEL, RINGS = range(11)


def kernel(rs_ref, widths_ref, first_ref, l_hbm, u_hbm, d_hbm, out_ref, scratch):
    row = lax.axis_index("row")
    col = lax.axis_index("col")
    x, z, core = row // 16, (row // 2) % 8, row % 2
    q = x * NZ + z
    other = 1 - core
    lw, uw, dw, sel, perm = (scratch[n] for n in ("lw", "uw", "dw", "sel", "perm"))
    fw, bw, pend, acc = (scratch[n] for n in ("fw", "bw", "pend", "acc"))
    rows_in, rows_out = scratch["rows_in"], scratch["rows_out"]
    gather, relay_sem, load_sem = scratch["gather"], scratch["relay_sem"], scratch["load_sem"]
    slabs, sums, ring_sem = scratch["slabs"], scratch["sums"], scratch["ring_sem"]
    panel, mpanel, split = scratch["panel"], scratch["mpanel"], scratch["split"]
    top1, top0, wide_u = scratch["top1"], scratch["top0"], scratch["wide_u"]
    place, packed = scratch["place"], scratch["packed"]

    loads = [
        pltpu.make_async_copy(src, dst, load_sem.at[i])
        for i, (src, dst) in enumerate(((l_hbm, lw), (u_hbm, uw), (d_hbm, dw)))
    ]
    for load in loads:
        load.start()

    barrier = pltpu.get_barrier_semaphore()

    def plane_peer(k):
        px, pz = (x + k // NZ) % NX, (z + k % NZ) % NZ
        return (px * NZ + pz) * 2 + core

    def signal(target):
        pl.semaphore_signal(barrier, inc=1, device_id=target, device_id_type=MESH)

    @pl.loop(1, NQ)
    def _(k):
        signal({"row": plane_peer(k)})

    @pl.loop(1, NC)
    def _(k):
        signal({"col": (col + k) % NC})

    signal({"row": q * 2 + other})

    def iota(shape, dim):
        return lax.broadcasted_iota(jnp.int32, shape, dim)

    def table(hit):
        return hit.astype(F32).astype(BF)

    def heap_row(r):
        s = r // 4
        n = jnp.where(s < 16, s + 15, jnp.where(s < 24, s - 9, jnp.where(s < 28, s - 21, s - 28)))
        return n * 4 + r % 4

    rows_out[...] = jnp.zeros_like(rows_out)
    rows_out[0:124] = rs_ref[...]
    order = table(iota((128, 128), 1) == heap_row(iota((128, 128), 0)))
    rows_in[...] = jnp.dot(order, rows_out[...], preferred_element_type=F32).astype(BF)

    row16 = iota((GROUP, 256), 0)
    own_row = row * 32 + col * 4 + row16 % 4

    def valid(t, g):
        limit = jnp.zeros((GROUP, 256), jnp.int32)
        for j in range(4):
            limit = jnp.where(row16 // 4 == j, widths_ref[2**t - 1 + 4 * g + j], limit)
        return (own_row < limit).astype(F32)

    def piece(t, g):
        at = (GBASE[t] + g) * GROUP
        return slice(at, at + GROUP)

    for g in range(4):
        y = valid(4, g) * rows_in[piece(4, g)].astype(F32)
        gather["f4"][g, core, q] = y.astype(BF)

    @pl.loop(0, 2)
    def _(h):
        @pl.loop(0, 8)
        def _(b):
            r = iota((128, 512), 0) + b * 128
            s = iota((128, 512), 1)
            p = (r % 256) // 4
            target = (p // 2) * 16 + (r // 256) * 4 + r % 4
            hit = jnp.logical_and(s == target, p % 2 == h)
            sel[h, pl.ds(pl.multiple_of(b * 128, 128), 128)] = table(hit)

    r, s = iota((128, 128), 0), iota((128, 128), 1)
    perm[...] = table(s == ((r // 4) % 4) * 32 + (r // 16) * 4 + r % 4)

    out_row = row * 32 + iota((32, 256), 0)
    lane = iota((32, 256), 1)
    in_row = (lane // 4) * 32 + col * 4 + lane % 4

    def mask(ref, index, t, hop):
        @pl.loop(0, 2**t)
        def _(n):
            keep = table(index >= first_ref[2**t - 1 + n, hop])
            ref[OFF[t, hop] + n] = ref[OFF[t, hop] + n] * keep

    def stack(ref, base, groups, members):
        return jnp.concatenate(
            [
                jnp.concatenate([ref[base + 4 * g + j] for j in members], axis=1)
                for g in range(groups)
            ],
            axis=0,
        )

    def expand(left, h, first, last):
        part = sel[h, first * 256 : last * 256]
        return jnp.dot(left, part, preferred_element_type=F32)

    def expand_forward(t):
        groups = GROUPS[t]
        for target, at, count in FROWS[t][0]:
            if target >= 0:
                hop = t - 1 - target
                halves = count // 32
                per = 4 // halves
                jobs = [
                    (lw, OFF[t, hop], at + 32 * v, [v * per + w for w in range(per)])
                    for v in range(halves)
                ]
            else:
                jobs = [(dw, 2**t - 1, at + 32 * j, [j]) for j in range(4)]
            for ref, base, first, members in jobs:
                left = stack(ref, base, groups, members)

                @pl.loop(0, 2)
                def _(h):
                    wide = expand(left, h, members[0], members[-1] + 1).astype(BF)
                    for g in range(groups):
                        fw[t][g, h, first : first + 32] = wide[g * 32 : (g + 1) * 32]

    def uppers(s, hop, first, count):
        base = OFF[s, hop] + first
        return uw[base : base + count].reshape(count * 32, 256)

    def expand_backward(t):
        for s, at, count in BROWS[t][0]:
            if t == 1:
                each = 2 ** (s - 1)
                for a in range(2):
                    root = uppers(s, s - 1, a * each, each)
                    parent = uppers(s, s - 2, a * each, each)
                    first = at + a * each * 32

                    @pl.loop(0, 2)
                    def _(h):
                        wide = expand(root, h, 0, 1) + expand(parent, h, 1 + a, 2 + a)
                        bw[t][0, h, first : first + each * 32] = wide.astype(BF)

                continue
            each = 2 ** (s - t)
            for g in range(GROUPS[t]):
                for j in range(4):
                    left = uppers(s, s - 1 - t, (4 * g + j) * each, each)
                    first = at + j * each * 32

                    @pl.loop(0, 2)
                    def _(h):
                        wide = expand(left, h, j, j + 1).astype(BF)
                        bw[t][g, h, first : first + each * 32] = wide

    def remote(src, dst, number, target):
        return pltpu.make_async_remote_copy(
            src_ref=src,
            dst_ref=dst,
            send_sem=relay_sem.at[0, number],
            recv_sem=relay_sem.at[1, number],
            device_id=target,
            device_id_type=MESH,
        )

    def spread(ref, number):
        @pl.loop(1, NQ)
        def _(k):
            mine = ref.at[core, q]
            remote(mine, mine, number, {"row": plane_peer(k)}).start()

    def spread_wait(ref, number):
        some = ref.at[core, 0 : NQ - 1]
        remote(some, some, number, {"row": q * 2 + other}).wait_recv()

    def share(ref, number):
        half = ref.at[core]
        remote(half, half, number, {"row": q * 2 + other}).start()

    def share_wait(ref, number):
        half = ref.at[other]
        remote(half, half, number, {"row": q * 2 + other}).wait_recv()

    def ring(src, dst, number, target):
        return pltpu.make_async_remote_copy(
            src_ref=src,
            dst_ref=dst,
            send_sem=ring_sem.at[0, number],
            recv_sem=ring_sem.at[1, number],
            device_id={"col": target},
            device_id_type=MESH,
        )

    def ring_all(landing, number):
        @pl.loop(1, NC)
        def _(k):
            mine = landing.at[col]
            ring(mine, mine, number, (col + k) % NC).start()

    def ring_wait(landing, number):
        some = landing.at[0 : NC - 1]
        ring(some, some, number, (col + 1) % NC).wait_recv()

    def reduce_start(source, t, number):
        for g in range(GROUPS[t]):
            part = source[g * 128 : (g + 1) * 128].astype(BF)
            cut = jnp.dot(perm[...], part, preferred_element_type=F32).astype(BF)
            slabs[number][:, g * GROUP : (g + 1) * GROUP] = cut.reshape(NC, GROUP, 256)
        reduce_send(number)

    def reduce_send(number):
        slab, landing = slabs[number], sums[number]

        @pl.loop(1, NC)
        def _(k):
            to = (col + k) % NC
            ring(slab.at[to], landing.at[col], number, to).start()

        landing[col] = slab[col]

    def reduced(number, at):
        landing = sums[number]
        total = landing[0, at].astype(F32)
        for k in range(1, NC):
            total = total + landing[k, at].astype(F32)
        return total

    lane_block = iota((8, 128), 1) // 32

    def pack(blocks):
        total = jnp.where(lane_block == 0, blocks[0], 0.0)
        for b in range(1, 4):
            total = total + jnp.where(lane_block == b, blocks[b], 0.0)
        return total

    def split_start(t, number):
        kind = slabs[number].dtype
        for u in range(2):
            for w in range(4):
                cut = []
                for n in range(2**t):
                    blocks = [
                        pend[t][n * 32 + b * 8 : n * 32 + b * 8 + 8, u * 128 : u * 128 + 128]
                        for b in range(4)
                    ]
                    blocks = [
                        v if b == w else pltpu.roll(v, ((b - w) * 32) % 128, 1)
                        for b, v in enumerate(blocks)
                    ]
                    cut.append(pack(blocks))
                whole = cut[0] if t == 0 else jnp.concatenate(cut, axis=0)
                slabs[number][4 * u + w] = whole.astype(kind)
        reduce_send(number)

    def valid_top(n):
        r = row * 32 + lane_block * 8 + iota((8, 128), 0)
        return (r < widths_ref[n]).astype(F32)

    def fold(wide):
        lanes = iota((32, 128), 1) // 32
        total = jnp.where(lanes == 0, wide[0:32], 0.0)
        for b in range(1, 4):
            total = total + jnp.where(lanes == b, wide[b * 32 : b * 32 + 32], 0.0)
        total = total + pltpu.roll(total, 64, 1)
        total = total + pltpu.roll(total, 32, 1)
        return pack([total[b * 8 : b * 8 + 8] for b in range(4)])

    def top_product(weights, ref, first, count):
        near = ref[core].reshape(NQ * GROUP, 128)
        far = ref[other].reshape(NQ * GROUP, 128)
        rows = slice(first, first + count)
        return jnp.dot(weights[core, rows], near, preferred_element_type=F32) + jnp.dot(
            weights[other, rows], far, preferred_element_type=F32
        )

    def panels(ref, index, b):
        return jnp.concatenate([ref[2 * b, index], ref[2 * b + 1, index]], axis=1)

    def block_of(ref, h, g):
        if ref.shape[2] == GROUP:
            return ref[h].reshape(NQ * GROUP, 256)
        return ref[h, :, g * GROUP : (g + 1) * GROUP].reshape(NQ * GROUP, 256)

    def add_forward(t, g, h, ref, entry, start):
        target, at, count = entry
        weights = fw[t][g, h, at : at + count]
        value = jnp.dot(weights, block_of(ref, h, g), preferred_element_type=F32)
        if target < 0:
            base = g * 128
            if start:
                acc[t][base : base + count] = value
            else:
                acc[t][base : base + count] += value
        else:
            first = ((4 * g) >> (t - target)) * 32
            pend[target][first : first + count] += value

    def add_backward(t, g, h, ref, entry):
        s, at, count = entry
        weights = bw[t][g, h, at : at + count]
        value = jnp.dot(weights, block_of(ref, h, g), preferred_element_type=F32)
        first = g * 128 * 2 ** (s - t)
        acc[s][first : first + count] -= value

    for load in loads:
        load.wait()
    mask(lw, out_row, 1, 0)
    mask(uw, in_row, 1, 0)
    for n in range(2):
        panel[col, TL + n] = lw[OFF[1, 0] + n]
        panel[col, TU + n] = uw[OFF[1, 0] + n]
    d0 = gather["d0"]
    inside = dw[0] * table(out_row < widths_ref[0])
    panel[col, TD] = inside
    for i in range(2):
        d0[i, core, q] = inside[i * GROUP : (i + 1) * GROUP]
    for n in range(1, 3):
        panel[col, TD + n] = dw[n]
    for t in range(4, 1, -1):
        for hop in range(t):
            mask(lw, out_row, t, hop)

    e, f = iota((96, GROUP), 0), iota((96, GROUP), 1)
    expanded = table(jnp.logical_and(e // 32 == f // 4, e % 32 == col * 4 + f % 4))
    begun = -jnp.dot(expanded, rows_in[piece(0, 0)], preferred_element_type=F32)
    pend[0][...] = begun[0:32]
    pend[1][...] = begun[32:96]
    for t in range(2, 4):
        pend[t][...] = jnp.zeros_like(pend[t])
    expand_forward(4)
    pl.semaphore_wait(barrier, NQ - 1 + NC - 1 + 1)

    f4 = gather["f4"]
    for g in range(4):

        @pl.loop(1, NZ)
        def _(k):
            mine = f4.at[g, core, q]
            remote(mine, mine, 3 * g, {"row": (x * NZ + (z + k) % NZ) * 2 + core}).start()

    ring_all(panel, PANEL)
    expand_forward(3)
    expand_forward(2)
    for g in range(4):
        some = f4.at[g, core, 0 : NZ - 1]
        remote(some, some, 3 * g, {"row": q * 2 + other}).wait_recv()

        @pl.loop(1, NX)
        def _(k):
            line = f4.at[g, core, pl.ds(x * NZ, NZ)]
            remote(line, line, 3 * g + 1, {"row": (((x + k) % NX) * NZ + z) * 2 + core}).start()

    for s in range(1, LEVELS):
        for hop in range(s):
            if s > 1:
                mask(uw, in_row, s, hop)
    @pl.loop(0, 8)
    def _(b):
        r, s = iota((128, 256), 0), iota((128, 256), 1)
        hit = jnp.logical_and(r // 32 == col // 2, s == b * 32 + r % 32)
        place[pl.ds(pl.multiple_of(b * 128, 128), 128)] = table(hit)

    parents = FROWS[4][0][0]
    for g in range(4):
        some = f4.at[g, core, 0 : NQ - NZ]
        remote(some, some, 3 * g + 1, {"row": q * 2 + other}).wait_recv()
        share(f4.at[g], 3 * g + 2)
        add_forward(4, g, core, f4.at[g], parents, True)
        if g > 0:
            share_wait(f4.at[g - 1], 3 * (g - 1) + 2)
            add_forward(4, g - 1, other, f4.at[g - 1], parents, False)
    share_wait(f4.at[3], 11)
    add_forward(4, 3, other, f4.at[3], parents, False)
    reduce_start(pend[3], 3, R3)
    spread(d0.at[0], 12)
    for g in range(4):
        for entry in FROWS[4][0][1:]:
            add_forward(4, g, core, f4.at[g], entry, True)
            add_forward(4, g, other, f4.at[g], entry, False)

    for t, number, ringed in ((3, 14, R3), (2, 16, R2)):
        ref = gather[f"f{t}"]
        ring_wait(sums[ringed], ringed)
        for g in range(GROUPS[t]):
            at = slice(g * GROUP, (g + 1) * GROUP)
            y = rows_in[piece(t, g)].astype(F32) - reduced(ringed, at)
            ref[core, q, at] = (valid(t, g) * y).astype(BF)
        spread(ref, number)
        if t == 3:
            ring_wait(panel, PANEL)
            for g in range(2):
                for n in range(2):
                    left = jnp.concatenate([panel[4 * g + j, TU + n] for j in range(4)], axis=1)

                    @pl.loop(0, 2)
                    def _(h):
                        wide_u[g, h, n * 32 : n * 32 + 32] = expand(left, h, 0, 4).astype(BF)

            left = jnp.concatenate(
                [
                    jnp.concatenate([panels(panel, TL, b), panels(panel, TL + 1, b)], axis=1)
                    for b in range(4)
                ],
                axis=0,
            )

            @pl.loop(0, 2)
            def _(h):
                top1[h, 0:128] = expand(left, h, 0, 4).astype(BF)

            for n in range(3):
                left = jnp.concatenate([panels(panel, TD + n, b) for b in range(4)], axis=0)

                @pl.loop(0, 2)
                def _(h):
                    if n == 0:
                        top0[h, 0:128] = expand(left, h, 0, 2).astype(BF)
                    else:
                        wide = expand(left, h, 2 * n - 2, 2 * n).astype(BF)
                        top1[h, n * 128 : n * 128 + 128] = wide

        else:
            expand_backward(1)
        spread_wait(ref, number)
        share(ref, number + 1)
        parents = FROWS[t][0][0]
        for g in range(GROUPS[t]):
            add_forward(t, g, core, ref, parents, True)
        share_wait(ref, number + 1)
        for g in range(GROUPS[t]):
            add_forward(t, g, other, ref, parents, False)
        if t == 3:
            reduce_start(pend[2], 2, R2)
            spread_wait(d0.at[0], 12)
            share(d0.at[0], 13)
            spread(d0.at[1], 18)
        else:
            split_start(1, P1)
        for g in range(GROUPS[t]):
            for entry in FROWS[t][0][1:]:
                add_forward(t, g, core, ref, entry, True)
                add_forward(t, g, other, ref, entry, False)

    split_start(0, P0)
    spread_wait(d0.at[1], 18)
    share(d0.at[1], 19)
    y1 = gather["y1"]
    ring_wait(sums[P1], P1)
    solved = -reduced(P1, slice(0, GROUP))
    for n in range(2):
        solved_n = valid_top(1 + n) * solved[n * 8 : n * 8 + 8]
        packed[n * 8 : n * 8 + 8] = solved_n
    y1[core, q] = packed[...].astype(BF)
    spread(y1, 20)
    share_wait(d0.at[0], 13)
    share_wait(d0.at[1], 19)
    product = jnp.zeros((64, 256), F32)
    for g in range(2):
        for h in range(2):
            product = product + jnp.dot(
                wide_u[g, h], d0[g, h].reshape(NQ * GROUP, 256), preferred_element_type=F32
            )
    mpanel[col] = product.astype(BF).reshape(2, 32, 256)
    ring_all(mpanel, MPANEL)
    expand_backward(2)
    ring_wait(sums[P0], P0)
    spread_wait(y1, 20)
    share(y1, 21)
    share_wait(y1, 21)
    y0 = -reduced(P0, slice(0, 8)) - fold(top_product(top1, y1, 0, 128))
    y0 = valid_top(0) * y0
    ref = gather["y0"]
    packed[0:8] = y0
    packed[8:16] = jnp.zeros((8, 128), F32)
    ref[core, q] = packed[...].astype(BF)
    spread(ref, 22)
    wide = top_product(top1, y1, 128, 256)
    scaled = [fold(wide[n * 128 : n * 128 + 128]) for n in range(2)]
    ring_wait(mpanel, MPANEL)
    for n in range(2):
        left = jnp.concatenate([panels(mpanel, n, b) for b in range(4)], axis=0)

        @pl.loop(0, 2)
        def _(h):
            wide = expand(left, h, 0, 2).astype(BF)
            top0[h, 128 + n * 128 : 256 + n * 128] = wide

    expand_backward(3)
    spread_wait(ref, 22)
    share(ref, 23)
    share_wait(ref, 23)
    wide = top_product(top0, ref, 0, 384)
    split[col, 0:8] = (valid_top(0) * fold(wide[0:128])).astype(BF)
    for n in range(2):
        s1 = scaled[n] - fold(wide[128 + n * 128 : 256 + n * 128])
        packed[n * 8 : n * 8 + 8] = valid_top(1 + n) * s1
    split[col, 8:24] = packed[...].astype(BF)
    split[col, 24:32] = jnp.zeros((8, 128), BF)
    ring_all(split, SPLIT)
    e, f = iota((GROUP, 32), 0), iota((GROUP, 32), 1)
    rows = table(f == (e // 4) * 8 + (col % 2) * 4 + e % 4)
    ring_wait(split, SPLIT)
    side = jnp.concatenate([split[k] for k in range(NC)], axis=1)
    side = jnp.dot(side, place[...], preferred_element_type=F32).astype(BF)
    solved = jnp.dot(rows, side, preferred_element_type=F32).astype(BF)
    rows_out[piece(0, 0)] = solved

    gather["b1"][core, q] = solved
    for t, number, ringed in ((1, 24, None), (2, 26, B2), (3, 28, B3), (4, None, B4)):
        if t > 1:
            ring_wait(sums[ringed], ringed)
            for g in range(GROUPS[t]):
                at = slice(g * GROUP, (g + 1) * GROUP)
                solved = (valid(t, g) * reduced(ringed, at)).astype(BF)
                rows_out[piece(t, g)] = solved
                if t < 4:
                    gather[f"b{t}"][core, q, at] = solved
        if t == 4:
            break
        ref = gather[f"b{t}"]
        spread(ref, number)
        spread_wait(ref, number)
        share(ref, number + 1)
        children = BROWS[t][0][0]
        for g in range(GROUPS[t]):
            add_backward(t, g, core, ref, children)
        share_wait(ref, number + 1)
        for g in range(GROUPS[t]):
            add_backward(t, g, other, ref, children)
        reduce_start(acc[t + 1], t + 1, {1: B2, 2: B3, 3: B4}[t])
        for g in range(GROUPS[t]):
            for entry in BROWS[t][0][1:]:
                add_backward(t, g, core, ref, entry)
                add_backward(t, g, other, ref, entry)

    order = table(iota((128, 128), 0) == heap_row(iota((128, 128), 1)))
    answer = jnp.dot(order, rows_out[...], preferred_element_type=F32).astype(BF)
    out_ref[...] = answer[0:124]

    for g in range(4):
        sent = f4.at[g, core, 0 : NZ - 1]
        remote(sent, sent, 3 * g, {"row": q * 2 + other}).wait_send()
        sent = f4.at[g, core, 0 : NQ - NZ]
        remote(sent, sent, 3 * g + 1, {"row": q * 2 + other}).wait_send()
        sent = f4.at[g, core]
        remote(sent, sent, 3 * g + 2, {"row": q * 2 + other}).wait_send()
    for ref, first, second in (
        (d0.at[0], 12, 13),
        (gather["f3"], 14, 15),
        (gather["f2"], 16, 17),
        (d0.at[1], 18, 19),
        (gather["y1"], 20, 21),
        (gather["y0"], 22, 23),
        (gather["b1"], 24, 25),
        (gather["b2"], 26, 27),
        (gather["b3"], 28, 29),
    ):
        sent = ref.at[core, 0 : NQ - 1]
        remote(sent, sent, first, {"row": q * 2 + other}).wait_send()
        sent = ref.at[core]
        remote(sent, sent, second, {"row": q * 2 + other}).wait_send()
    for number in range(RINGS):
        landing = {SPLIT: split, PANEL: panel, MPANEL: mpanel}.get(number)
        landing = sums[number] if landing is None else landing
        sent = landing.at[0 : NC - 1]
        ring(sent, sent, number, (col + 1) % NC).wait_send()


def scratch_shapes():
    gather = {
        "f4": pltpu.VMEM((4, 2, NQ, GROUP, 256), BF),
        "d0": pltpu.VMEM((2, 2, NQ, GROUP, 256), BF),
        "y1": pltpu.VMEM((2, NQ, GROUP, 128), BF),
        "y0": pltpu.VMEM((2, NQ, GROUP, 128), BF),
    }
    for name, t in (("f3", 3), ("f2", 2), ("b1", 1), ("b2", 2), ("b3", 3)):
        gather[name] = pltpu.VMEM((2, NQ, GROUP * GROUPS[t], 256), BF)
    slabs = {n: pltpu.VMEM((NC, GROUP * k, 256), BF) for n, k in ((R3, 2), (R2, 1), (B2, 1), (B3, 2), (B4, 4))}
    slabs[P1] = pltpu.VMEM((NC, GROUP, 128), BF)
    slabs[P0] = pltpu.VMEM((NC, 8, 128), F32)
    return {
        "lw": pltpu.VMEM((98, 32, 256), BF),
        "uw": pltpu.VMEM((98, 32, 256), BF),
        "dw": pltpu.VMEM((31, 32, 256), BF),
        "rows_in": pltpu.VMEM((128, 256), BF),
        "rows_out": pltpu.VMEM((128, 256), BF),
        "sel": pltpu.VMEM((2, 1024, 512), BF),
        "perm": pltpu.VMEM((128, 128), BF),
        "place": pltpu.VMEM((1024, 256), BF),
        "packed": pltpu.VMEM((GROUP, 128), F32),
        "fw": {t: pltpu.VMEM((GROUPS[t], 2, FROWS[t][1], 512), BF) for t in FROWS},
        "bw": {t: pltpu.VMEM((GROUPS[t], 2, BROWS[t][1], 512), BF) for t in BROWS},
        "top1": pltpu.VMEM((2, 384, 512), BF),
        "top0": pltpu.VMEM((2, 384, 512), BF),
        "wide_u": pltpu.VMEM((2, 2, 64, 512), BF),
        "panel": pltpu.VMEM((NC, TOPS, 32, 256), BF),
        "mpanel": pltpu.VMEM((NC, 2, 32, 256), BF),
        "split": pltpu.VMEM((NC, 32, 128), BF),
        "pend": [pltpu.VMEM((32 * 2**t, 256), F32) for t in range(4)],
        "acc": {t: pltpu.VMEM((32 * 2**t, 256), F32) for t in range(TOP, LEVELS)},
        "gather": gather,
        "slabs": slabs,
        "sums": dict(slabs),
        "relay_sem": pltpu.SemaphoreType.DMA((2, 30)),
        "ring_sem": pltpu.SemaphoreType.DMA((2, RINGS)),
        "load_sem": pltpu.SemaphoreType.DMA((3,)),
    }


def shards(right_side, lower_blocks, upper_blocks, pivot_inverse, widths, first_row):
    nodes, rows, columns = right_side.shape
    vmem = pl.BlockSpec(memory_space=pltpu.VMEM)
    smem = pl.BlockSpec(memory_space=pltpu.SMEM)
    hbm = pl.BlockSpec(memory_space=pl.ANY)
    leaves, tree = jax.tree.flatten(scratch_shapes())

    def body(*refs):
        kernel(*refs[:7], jax.tree.unflatten(tree, refs[7:]))

    answer = pl.pallas_call(
        body,
        out_shape=jax.ShapeDtypeStruct((nodes * rows, columns), BF),
        in_specs=[vmem, smem, smem, hbm, hbm, hbm],
        out_specs=vmem,
        scratch_shapes=leaves,
        compiler_params=pltpu.CompilerParams(
            collective_id=1, has_side_effects=True, vmem_limit_bytes=56 * 1024 * 1024
        ),
        name="tree_solve",
    )(
        right_side.reshape(nodes * rows, columns),
        widths,
        first_row,
        lower_blocks,
        upper_blocks,
        pivot_inverse,
    )
    return answer.reshape(nodes, rows, columns)


def solution(mesh):
    in_specs = (
        P(None, ("row", "col"), None),
        P(None, "row", "col"),
        P(None, "row", "col"),
        P(None, "row", "col"),
        P(),
        P(),
    )
    out_specs = P(None, ("row", "col"), None)
    return jax.shard_map(shards, mesh=mesh, in_specs=in_specs, out_specs=out_specs, check_vma=False)
```

```python
import functools

import jax
import jax.numpy as jnp
from jax import lax
from jax.experimental import pallas as pl
from jax.experimental.pallas import tpu as pltpu
from jax.sharding import PartitionSpec as P

MESH = pl.DeviceIdType.MESH
BF = jnp.bfloat16
F32 = jnp.float32
LEVELS = 5
NX, NZ, NC = 4, 8, 8
NQ = NX * NZ
TOP = 2
GROUPS = [1, 1, 1, 2, 4]
GBASE = [7, 7, 6, 4, 0]
NGROUP = 8
GROUP = 16


def block_offsets():
    offsets = {}
    running = 0
    for tree_level in range(1, LEVELS):
        for hop_up in range(tree_level):
            offsets[tree_level, hop_up] = running
            running = running + 2**tree_level
    return offsets


OFF = block_offsets()


def forward_rows(t):
    rows, at = [], 0
    for hop in range(t):
        count = 64 if hop == 0 else 32
        rows.append((t - 1 - hop, at, count))
        at += count
    rows.append((-1, at, 128))
    return rows, at + 128


def backward_rows(t):
    rows, at = [], 0
    for s in range(t + 1, LEVELS):
        count = 32 * (2**s if t == 1 else 4 * 2 ** (s - t))
        rows.append((s, at, count))
        at += count
    return rows, at


FROWS = {t: forward_rows(t) for t in range(TOP, LEVELS)}
BROWS = {t: backward_rows(t) for t in range(1, LEVELS - 1)}
TL, TU, TD, TOPS = 0, 2, 4, 7
R3, R2, P1, P0, SPLIT, B2, B3, B4, PANEL, MPANEL, RINGS = range(11)


def kernel(rs_ref, widths_ref, first_ref, l_hbm, u_hbm, d_hbm, out_ref, scratch):
    row = lax.axis_index("row")
    col = lax.axis_index("col")
    x, z, core = row // 16, (row // 2) % 8, row % 2
    q = x * NZ + z
    other = 1 - core
    lw, uw, dw, sel, perm = (scratch[n] for n in ("lw", "uw", "dw", "sel", "perm"))
    fw, bw, pend, acc = (scratch[n] for n in ("fw", "bw", "pend", "acc"))
    rows_in, rows_out, heap = (scratch[n] for n in ("rows_in", "rows_out", "heap"))
    gather, relay_sem, load_sem = scratch["gather"], scratch["relay_sem"], scratch["load_sem"]
    slabs, sums, ring_sem = scratch["slabs"], scratch["sums"], scratch["ring_sem"]
    panel, mpanel, split = scratch["panel"], scratch["mpanel"], scratch["split"]
    top1, top0, wide_u = scratch["top1"], scratch["top0"], scratch["wide_u"]
    place, packed = scratch["place"], scratch["packed"]

    loads = [
        pltpu.make_async_copy(src, dst, load_sem.at[i])
        for i, (src, dst) in enumerate(((l_hbm, lw), (u_hbm, uw), (d_hbm, dw)))
    ]
    for load in loads:
        load.start()

    barrier = pltpu.get_barrier_semaphore()

    def away(k, n):
        return (n // 2 + (k + 1) // 2 * (1 - 2 * ((k + 1) % 2))) % n

    def plane_peer(k):
        px, pz = (x + away(k % NX, NX)) % NX, (z + away(k // NX, NZ)) % NZ
        return (px * NZ + pz) * 2 + core

    def signal(target):
        pl.semaphore_signal(barrier, inc=1, device_id=target, device_id_type=MESH)

    @pl.loop(0, NQ - 1)
    def _(k):
        signal({"row": plane_peer(k)})

    @pl.loop(0, NC - 1)
    def _(k):
        signal({"col": (col + away(k, NC)) % NC})

    signal({"row": q * 2 + other})

    def iota(shape, dim):
        return lax.broadcasted_iota(jnp.int32, shape, dim)

    def table(hit):
        return hit.astype(F32).astype(BF)

    def heap_row(r):
        s = r // 4
        n = jnp.where(s < 16, s + 15, jnp.where(s < 24, s - 9, jnp.where(s < 28, s - 21, s - 28)))
        return n * 4 + r % 4

    heap[124:128] = jnp.zeros((4, 256), F32)
    for n in range(31):
        heap[4 * n : 4 * n + 4] = rs_ref[n].astype(F32)
    order = table(iota((128, 128), 1) == heap_row(iota((128, 128), 0)))
    rows_in[...] = jnp.dot(order, heap[...].astype(BF), preferred_element_type=F32).astype(BF)

    row16 = iota((GROUP, 256), 0)
    own_row = row * 32 + col * 4 + row16 % 4

    def valid(t, g):
        limit = jnp.zeros((GROUP, 256), jnp.int32)
        for j in range(4):
            limit = jnp.where(row16 // 4 == j, widths_ref[2**t - 1 + 4 * g + j], limit)
        return (own_row < limit).astype(F32)

    def piece(t, g):
        at = (GBASE[t] + g) * GROUP
        return slice(at, at + GROUP)

    for g in range(4):
        y = valid(4, g) * rows_in[piece(4, g)].astype(F32)
        gather["f4"][g, core, x, z] = y.astype(BF)

    @pl.loop(0, 2)
    def _(h):
        @pl.loop(0, 8)
        def _(b):
            r = iota((128, 512), 0) + b * 128
            s = iota((128, 512), 1)
            p = (r % 256) // 4
            target = (p // 2) * 16 + (r // 256) * 4 + r % 4
            hit = jnp.logical_and(s == target, p % 2 == h)
            sel[h, pl.ds(pl.multiple_of(b * 128, 128), 128)] = table(hit)

    r, s = iota((128, 128), 0), iota((128, 128), 1)
    perm[...] = table(s == ((r // 4) % 4) * 32 + (r // 16) * 4 + r % 4)

    out_row = row * 32 + iota((32, 256), 0)
    lane = iota((32, 256), 1)
    in_row = (lane // 4) * 32 + col * 4 + lane % 4

    def mask(ref, index, t, hop):
        @pl.loop(0, 2**t)
        def _(n):
            keep = table(index >= first_ref[hop, 2**t - 1 + n])
            ref[OFF[t, hop] + n] = ref[OFF[t, hop] + n] * keep

    def stack(ref, base, groups, members):
        return jnp.concatenate(
            [
                jnp.concatenate([ref[base + 4 * g + j] for j in members], axis=1)
                for g in range(groups)
            ],
            axis=0,
        )

    def expand(left, h, first, last):
        part = sel[h, first * 256 : last * 256]
        return jnp.dot(left, part, preferred_element_type=F32)

    def expand_forward(t, entries):
        groups = GROUPS[t]
        for target, at, count in entries:
            if target >= 0:
                hop = t - 1 - target
                halves = count // 32
                per = 4 // halves
                jobs = [
                    (lw, OFF[t, hop], at + 32 * v, [v * per + w for w in range(per)])
                    for v in range(halves)
                ]
            else:
                jobs = [(dw, 2**t - 1, at + 32 * j, [j]) for j in range(4)]
            for ref, base, first, members in jobs:
                left = stack(ref, base, groups, members)

                @pl.loop(0, 2)
                def _(h):
                    wide = expand(left, h, members[0], members[-1] + 1).astype(BF)
                    for g in range(groups):
                        fw[t][g, h, first : first + 32] = wide[g * 32 : (g + 1) * 32]

    def uppers(s, hop, first, count):
        base = OFF[s, hop] + first
        return uw[base : base + count].reshape(count * 32, 256)

    def expand_backward(t):
        for s, at, count in BROWS[t][0]:
            if t == 1:
                each = 2 ** (s - 1)
                for a in range(2):
                    root = uppers(s, s - 1, a * each, each)
                    parent = uppers(s, s - 2, a * each, each)
                    first = at + a * each * 32

                    @pl.loop(0, 2)
                    def _(h):
                        wide = expand(root, h, 0, 1) + expand(parent, h, 1 + a, 2 + a)
                        bw[t][0, h, first : first + each * 32] = wide.astype(BF)

                continue
            each = 2 ** (s - t)
            for g in range(GROUPS[t]):
                for j in range(4):
                    left = uppers(s, s - 1 - t, (4 * g + j) * each, each)
                    first = at + j * each * 32

                    @pl.loop(0, 2)
                    def _(h):
                        wide = expand(left, h, j, j + 1).astype(BF)
                        bw[t][g, h, first : first + each * 32] = wide

    leaving = []

    def remote(src, dst, number, target):
        return pltpu.make_async_remote_copy(
            src_ref=src,
            dst_ref=dst,
            send_sem=relay_sem.at[0, number],
            recv_sem=relay_sem.at[1, number],
            device_id=target,
            device_id_type=MESH,
        )

    def spread(ref, number):
        @pl.loop(0, NQ - 1)
        def _(k):
            mine = ref.at[core, q]
            remote(mine, mine, number, {"row": plane_peer(k)}).start()

        leaving.append((remote, ref.at[core, 0 : NQ - 1], number, {"row": q * 2 + other}))

    def spread_wait(ref, number):
        some = ref.at[core, 0 : NQ - 1]
        remote(some, some, number, {"row": q * 2 + other}).wait_recv()

    def along_z(mine, some, number):
        @pl.loop(0, NZ - 1)
        def _(k):
            to = (x * NZ + (z + away(k, NZ)) % NZ) * 2 + core
            remote(mine, mine, number, {"row": to}).start()

        leaving.append((remote, some, number, {"row": q * 2 + other}))

    def along_x(mine, some, number):
        @pl.loop(0, NX - 1)
        def _(k):
            to = (((x + away(k, NX)) % NX) * NZ + z) * 2 + core
            remote(mine, mine, number, {"row": to}).start()

        leaving.append((remote, some, number, {"row": q * 2 + other}))

    def landed(some, number):
        remote(some, some, number, {"row": q * 2 + other}).wait_recv()

    def z_first(ref, number):
        along_z(ref.at[core, x, z], ref.at[core, 0, 0 : NZ - 1], number)

    def then_x(ref, number):
        landed(ref.at[core, 0, 0 : NZ - 1], number)
        along_x(ref.at[core, x], ref.at[core, 0 : NX - 1], number + 1)

    def x_landed(ref, number):
        landed(ref.at[core, 0 : NX - 1], number + 1)

    def x_first(ref, number):
        along_x(ref.at[core, x, z], ref.at[core, 0, 0 : NX - 1], number)

    def then_z(ref, number):
        landed(ref.at[core, 0, 0 : NX - 1], number)
        along_z(ref.at[core, :, z], ref.at[core, :, 0 : NZ - 1], number + 1)

    def z_landed(ref, number):
        landed(ref.at[core, :, 0 : NZ - 1], number + 1)

    def share(ref, number):
        half = ref.at[core]
        remote(half, half, number, {"row": q * 2 + other}).start()
        leaving.append((remote, half, number, {"row": q * 2 + other}))

    def share_wait(ref, number):
        half = ref.at[other]
        remote(half, half, number, {"row": q * 2 + other}).wait_recv()

    def ring(src, dst, number, target):
        return pltpu.make_async_remote_copy(
            src_ref=src,
            dst_ref=dst,
            send_sem=ring_sem.at[0, number],
            recv_sem=ring_sem.at[1, number],
            device_id={"col": target},
            device_id_type=MESH,
        )

    def ring_all(landing, number):
        @pl.loop(0, NC - 1)
        def _(k):
            mine = landing.at[col]
            ring(mine, mine, number, (col + away(k, NC)) % NC).start()

        leaving.append((ring, landing.at[0 : NC - 1], number, (col + 1) % NC))

    def ring_wait(landing, number):
        some = landing.at[0 : NC - 1]
        ring(some, some, number, (col + 1) % NC).wait_recv()

    def reduce_start(source, t, number):
        for g in range(GROUPS[t]):
            part = source[g * 128 : (g + 1) * 128].astype(BF)
            cut = jnp.dot(perm[...], part, preferred_element_type=F32).astype(BF)
            slabs[number][:, g * GROUP : (g + 1) * GROUP] = cut.reshape(NC, GROUP, 256)
        reduce_send(number)

    def reduce_send(number):
        slab, landing = slabs[number], sums[number]

        @pl.loop(0, NC - 1)
        def _(k):
            to = (col + away(k, NC)) % NC
            ring(slab.at[to], landing.at[col], number, to).start()

        leaving.append((ring, landing.at[0 : NC - 1], number, (col + 1) % NC))
        landing[col] = slab[col]

    def reduced(number, at):
        landing = sums[number]
        total = landing[0, at].astype(F32)
        for k in range(1, NC):
            total = total + landing[k, at].astype(F32)
        return total

    lane_block = iota((8, 128), 1) // 32

    def pack(blocks):
        total = jnp.where(lane_block == 0, blocks[0], 0.0)
        for b in range(1, 4):
            total = total + jnp.where(lane_block == b, blocks[b], 0.0)
        return total

    def split_start(t, number):
        kind = slabs[number].dtype
        for u in range(2):
            for w in range(4):
                cut = []
                for n in range(2**t):
                    blocks = [
                        pend[t][n * 32 + b * 8 : n * 32 + b * 8 + 8, u * 128 : u * 128 + 128]
                        for b in range(4)
                    ]
                    blocks = [
                        v if b == w else pltpu.roll(v, ((b - w) * 32) % 128, 1)
                        for b, v in enumerate(blocks)
                    ]
                    cut.append(pack(blocks))
                whole = cut[0] if t == 0 else jnp.concatenate(cut, axis=0)
                slabs[number][4 * u + w] = whole.astype(kind)
        reduce_send(number)

    def valid_top(n):
        r = row * 32 + lane_block * 8 + iota((8, 128), 0)
        return (r < widths_ref[n]).astype(F32)

    def fold(wide):
        lanes = iota((32, 128), 1) // 32
        total = jnp.where(lanes == 0, wide[0:32], 0.0)
        for b in range(1, 4):
            total = total + jnp.where(lanes == b, wide[b * 32 : b * 32 + 32], 0.0)
        total = total + pltpu.roll(total, 64, 1)
        total = total + pltpu.roll(total, 32, 1)
        return pack([total[b * 8 : b * 8 + 8] for b in range(4)])

    def top_product(weights, ref, first, count):
        near = ref[core].reshape(NQ * GROUP, 128)
        far = ref[other].reshape(NQ * GROUP, 128)
        rows = slice(first, first + count)
        return jnp.dot(weights[core, rows], near, preferred_element_type=F32) + jnp.dot(
            weights[other, rows], far, preferred_element_type=F32
        )

    def panels(ref, index, b):
        return jnp.concatenate([ref[2 * b, index], ref[2 * b + 1, index]], axis=1)

    def add_forward(t, g, h, ref, entry, start):
        target, at, count = entry
        weights = fw[t][g, h, at : at + count]
        value = jnp.dot(weights, ref[h].reshape(NQ * GROUP, 256), preferred_element_type=F32)
        if target < 0:
            base = g * 128
            if start:
                acc[t][base : base + count] = value
            else:
                acc[t][base : base + count] += value
        else:
            first = ((4 * g) >> (t - target)) * 32
            pend[target][first : first + count] += value

    def add_backward(t, g, h, ref, entry):
        s, at, count = entry
        weights = bw[t][g, h, at : at + count]
        value = jnp.dot(weights, ref[h].reshape(NQ * GROUP, 256), preferred_element_type=F32)
        first = g * 128 * 2 ** (s - t)
        acc[s][first : first + count] -= value

    for load in loads:
        load.wait()
    mask(lw, out_row, 1, 0)
    mask(uw, in_row, 1, 0)
    for n in range(2):
        panel[col, TL + n] = lw[OFF[1, 0] + n]
        panel[col, TU + n] = uw[OFF[1, 0] + n]
    d0 = gather["d0"]
    inside = dw[0] * table(out_row < widths_ref[0])
    panel[col, TD] = inside
    d0[core, x, z] = inside
    for n in range(1, 3):
        panel[col, TD + n] = dw[n]
    pl.semaphore_wait(barrier, NQ - 1 + NC - 1 + 1)

    f4, f3, b3 = gather["f4"], gather["f3"], gather["b3"]
    x_first(f4.at[3], 9)
    for g in range(3):
        z_first(f4.at[g], 3 * g)
    ring_all(panel, PANEL)

    e, f = iota((96, GROUP), 0), iota((96, GROUP), 1)
    expanded = table(jnp.logical_and(e // 32 == f // 4, e % 32 == col * 4 + f % 4))
    begun = -jnp.dot(expanded, rows_in[piece(0, 0)], preferred_element_type=F32)
    pend[0][...] = begun[0:32]
    pend[1][...] = begun[32:96]
    for t in range(2, 4):
        pend[t][...] = jnp.zeros_like(pend[t])
    mask(lw, out_row, 4, 0)
    expand_forward(4, FROWS[4][0][:1])
    then_z(f4.at[3], 9)
    for t in range(4, 1, -1):
        for hop in range(t):
            if (t, hop) != (4, 0):
                mask(lw, out_row, t, hop)
    then_x(f4.at[0], 0)
    expand_forward(4, FROWS[4][0][1:3])
    then_x(f4.at[1], 3)
    then_x(f4.at[2], 6)
    z_first(d0, 12)
    expand_forward(4, FROWS[4][0][3:])
    x_landed(f4.at[0], 0)
    share(f4.at[0], 2)
    expand_forward(3, FROWS[3][0])

    parents = FROWS[4][0][0]
    for g in range(4):
        if g > 0:
            (x_landed if g < 3 else z_landed)(f4.at[g], 3 * g)
            share(f4.at[g], 3 * g + 2)
        add_forward(4, g, core, f4.at[g], parents, True)
        if g > 0:
            share_wait(f4.at[g - 1], 3 * (g - 1) + 2)
            add_forward(4, g - 1, other, f4.at[g - 1], parents, False)
    share_wait(f4.at[3], 11)
    add_forward(4, 3, other, f4.at[3], parents, False)
    reduce_start(pend[3], 3, R3)
    then_x(d0, 12)
    for g in range(4):
        for entry in FROWS[4][0][1:]:
            add_forward(4, g, core, f4.at[g], entry, True)
            add_forward(4, g, other, f4.at[g], entry, False)

    ring_wait(sums[R3], R3)
    for g in range(2):
        y = rows_in[piece(3, g)].astype(F32) - reduced(R3, slice(g * GROUP, (g + 1) * GROUP))
        f3[g, core, x, z] = (valid(3, g) * y).astype(BF)
    x_first(f3.at[1], 17)
    z_first(f3.at[0], 14)
    expand_forward(2, FROWS[2][0])
    then_z(f3.at[1], 17)
    ring_wait(panel, PANEL)
    left = jnp.concatenate(
        [
            jnp.concatenate([panels(panel, TL, b), panels(panel, TL + 1, b)], axis=1)
            for b in range(4)
        ],
        axis=0,
    )

    @pl.loop(0, 2)
    def _(h):
        top1[h, 0:128] = expand(left, h, 0, 4).astype(BF)

    then_x(f3.at[0], 14)
    x_landed(d0, 12)
    share(d0, 32)
    for g in range(2):
        left = jnp.concatenate(
            [
                jnp.concatenate([panel[4 * g + j, TU + n] for j in range(4)], axis=1)
                for n in range(2)
            ],
            axis=0,
        )

        @pl.loop(0, 2)
        def _(h):
            wide_u[g, h] = expand(left, h, 0, 4).astype(BF)

    for n in range(3):
        left = jnp.concatenate([panels(panel, TD + n, b) for b in range(4)], axis=0)

        @pl.loop(0, 2)
        def _(h):
            if n == 0:
                top0[h, 0:128] = expand(left, h, 0, 2).astype(BF)
            else:
                wide = expand(left, h, 2 * n - 2, 2 * n).astype(BF)
                top1[h, n * 128 : n * 128 + 128] = wide

    parents = FROWS[3][0][0]
    x_landed(f3.at[0], 14)
    share(f3.at[0], 16)
    add_forward(3, 0, core, f3.at[0], parents, True)
    z_landed(f3.at[1], 17)
    share(f3.at[1], 19)
    share_wait(f3.at[0], 16)
    add_forward(3, 0, other, f3.at[0], parents, False)
    add_forward(3, 1, core, f3.at[1], parents, True)
    share_wait(f3.at[1], 19)
    add_forward(3, 1, other, f3.at[1], parents, False)
    reduce_start(pend[2], 2, R2)
    for g in range(2):
        for entry in FROWS[3][0][1:]:
            add_forward(3, g, core, f3.at[g], entry, True)
            add_forward(3, g, other, f3.at[g], entry, False)
    share_wait(d0, 32)
    product = jnp.zeros((64, 256), F32)
    for g in range(2):
        for h in range(2):
            block = d0[h, :, :, g * GROUP : (g + 1) * GROUP].reshape(NQ * GROUP, 256)
            product = product + jnp.dot(wide_u[g, h], block, preferred_element_type=F32)
    mpanel[col] = product.astype(BF).reshape(2, 32, 256)

    ref = gather["f2"]
    ring_wait(sums[R2], R2)
    y = rows_in[piece(2, 0)].astype(F32) - reduced(R2, slice(0, GROUP))
    ref[core, q] = (valid(2, 0) * y).astype(BF)
    spread(ref, 20)
    ring_all(mpanel, MPANEL)
    for s in range(2, LEVELS):
        for hop in range(s):
            mask(uw, in_row, s, hop)
    expand_backward(1)
    spread_wait(ref, 20)
    share(ref, 21)
    parents = FROWS[2][0][0]
    add_forward(2, 0, core, ref, parents, True)
    share_wait(ref, 21)
    add_forward(2, 0, other, ref, parents, False)
    split_start(1, P1)
    for entry in FROWS[2][0][1:]:
        add_forward(2, 0, core, ref, entry, True)
        add_forward(2, 0, other, ref, entry, False)

    split_start(0, P0)
    @pl.loop(0, 8)
    def _(b):
        r, s = iota((128, 256), 0), iota((128, 256), 1)
        hit = jnp.logical_and(r // 32 == col // 2, s == b * 32 + r % 32)
        place[pl.ds(pl.multiple_of(b * 128, 128), 128)] = table(hit)

    y1 = gather["y1"]
    ring_wait(sums[P1], P1)
    solved = -reduced(P1, slice(0, GROUP))
    for n in range(2):
        packed[n * 8 : n * 8 + 8] = valid_top(1 + n) * solved[n * 8 : n * 8 + 8]
    y1[core, q] = packed[...].astype(BF)
    spread(y1, 22)
    expand_backward(2)
    ring_wait(sums[P0], P0)
    spread_wait(y1, 22)
    share(y1, 23)
    share_wait(y1, 23)
    y0 = -reduced(P0, slice(0, 8)) - fold(top_product(top1, y1, 0, 128))
    y0 = valid_top(0) * y0
    ref = gather["y0"]
    packed[0:8] = y0
    packed[8:16] = jnp.zeros((8, 128), F32)
    ref[core, q] = packed[...].astype(BF)
    spread(ref, 24)
    wide = top_product(top1, y1, 128, 256)
    scaled = [fold(wide[n * 128 : n * 128 + 128]) for n in range(2)]
    ring_wait(mpanel, MPANEL)
    for n in range(2):
        left = jnp.concatenate([panels(mpanel, n, b) for b in range(4)], axis=0)

        @pl.loop(0, 2)
        def _(h):
            wide = expand(left, h, 0, 2).astype(BF)
            top0[h, 128 + n * 128 : 256 + n * 128] = wide

    expand_backward(3)
    spread_wait(ref, 24)
    share(ref, 25)
    share_wait(ref, 25)
    wide = top_product(top0, ref, 0, 384)
    split[col, 0:8] = (valid_top(0) * fold(wide[0:128])).astype(BF)
    for n in range(2):
        s1 = scaled[n] - fold(wide[128 + n * 128 : 256 + n * 128])
        packed[n * 8 : n * 8 + 8] = valid_top(1 + n) * s1
    split[col, 8:24] = packed[...].astype(BF)
    split[col, 24:32] = jnp.zeros((8, 128), BF)
    ring_all(split, SPLIT)
    e, f = iota((GROUP, 32), 0), iota((GROUP, 32), 1)
    rows = table(f == (e // 4) * 8 + (col % 2) * 4 + e % 4)
    ring_wait(split, SPLIT)
    side = jnp.concatenate([split[k] for k in range(NC)], axis=1)
    side = jnp.dot(side, place[...], preferred_element_type=F32).astype(BF)
    solved = jnp.dot(rows, side, preferred_element_type=F32).astype(BF)
    rows_out[piece(0, 0)] = solved

    gather["b1"][core, q] = solved
    for t, number, ringed in ((1, 26, None), (2, 28, B2)):
        ref = gather[f"b{t}"]
        if t == 2:
            ring_wait(sums[B2], B2)
            solved = (valid(2, 0) * reduced(B2, slice(0, GROUP))).astype(BF)
            rows_out[piece(2, 0)] = solved
            ref[core, q] = solved
        spread(ref, number)
        spread_wait(ref, number)
        share(ref, number + 1)
        children = BROWS[t][0][0]
        add_backward(t, 0, core, ref, children)
        share_wait(ref, number + 1)
        add_backward(t, 0, other, ref, children)
        reduce_start(acc[t + 1], t + 1, {1: B2, 2: B3}[t])
        for entry in BROWS[t][0][1:]:
            add_backward(t, 0, core, ref, entry)
            add_backward(t, 0, other, ref, entry)
    ring_wait(sums[B3], B3)
    for g in range(2):
        solved = (valid(3, g) * reduced(B3, slice(g * GROUP, (g + 1) * GROUP))).astype(BF)
        rows_out[piece(3, g)] = solved
        b3[g, core, x, z] = solved
    x_first(b3.at[1], 33)
    z_first(b3.at[0], 30)
    then_z(b3.at[1], 33)
    then_x(b3.at[0], 30)
    children = BROWS[3][0][0]
    x_landed(b3.at[0], 30)
    share(b3.at[0], 35)
    add_backward(3, 0, core, b3.at[0], children)
    z_landed(b3.at[1], 33)
    share(b3.at[1], 36)
    share_wait(b3.at[0], 35)
    add_backward(3, 0, other, b3.at[0], children)
    add_backward(3, 1, core, b3.at[1], children)
    share_wait(b3.at[1], 36)
    add_backward(3, 1, other, b3.at[1], children)
    reduce_start(acc[4], 4, B4)
    ring_wait(sums[B4], B4)
    for g in range(4):
        solved = valid(4, g) * reduced(B4, slice(g * GROUP, (g + 1) * GROUP))
        rows_out[piece(4, g)] = solved.astype(BF)

    order = table(iota((128, 128), 0) == heap_row(iota((128, 128), 1)))
    heap[...] = jnp.dot(order, rows_out[...], preferred_element_type=F32)
    for n in range(31):
        out_ref[n] = heap[4 * n : 4 * n + 4].astype(BF)

    for kind, ref, number, target in leaving:
        kind(ref, ref, number, target).wait_send()


def scratch_shapes():
    gather = {
        "f4": pltpu.VMEM((4, 2, NX, NZ, GROUP, 256), BF),
        "f3": pltpu.VMEM((2, 2, NX, NZ, GROUP, 256), BF),
        "b3": pltpu.VMEM((2, 2, NX, NZ, GROUP, 256), BF),
        "d0": pltpu.VMEM((2, NX, NZ, 2 * GROUP, 256), BF),
        "y1": pltpu.VMEM((2, NQ, GROUP, 128), BF),
        "y0": pltpu.VMEM((2, NQ, GROUP, 128), BF),
    }
    for name in ("f2", "b1", "b2"):
        gather[name] = pltpu.VMEM((2, NQ, GROUP, 256), BF)
    slabs = {n: pltpu.VMEM((NC, GROUP * k, 256), BF) for n, k in ((R3, 2), (R2, 1), (B2, 1), (B3, 2), (B4, 4))}
    slabs[P1] = pltpu.VMEM((NC, GROUP, 128), BF)
    slabs[P0] = pltpu.VMEM((NC, 8, 128), F32)
    return {
        "lw": pltpu.VMEM((98, 32, 256), BF),
        "uw": pltpu.VMEM((98, 32, 256), BF),
        "dw": pltpu.VMEM((31, 32, 256), BF),
        "rows_in": pltpu.VMEM((128, 256), BF),
        "rows_out": pltpu.VMEM((128, 256), BF),
        "heap": pltpu.VMEM((128, 256), F32),
        "sel": pltpu.VMEM((2, 1024, 512), BF),
        "perm": pltpu.VMEM((128, 128), BF),
        "place": pltpu.VMEM((1024, 256), BF),
        "packed": pltpu.VMEM((GROUP, 128), F32),
        "fw": {t: pltpu.VMEM((GROUPS[t], 2, FROWS[t][1], 512), BF) for t in FROWS},
        "bw": {t: pltpu.VMEM((GROUPS[t], 2, BROWS[t][1], 512), BF) for t in BROWS},
        "top1": pltpu.VMEM((2, 384, 512), BF),
        "top0": pltpu.VMEM((2, 384, 512), BF),
        "wide_u": pltpu.VMEM((2, 2, 64, 512), BF),
        "panel": pltpu.VMEM((NC, TOPS, 32, 256), BF),
        "mpanel": pltpu.VMEM((NC, 2, 32, 256), BF),
        "split": pltpu.VMEM((NC, 32, 128), BF),
        "pend": [pltpu.VMEM((32 * 2**t, 256), F32) for t in range(4)],
        "acc": {t: pltpu.VMEM((32 * 2**t, 256), F32) for t in range(TOP, LEVELS)},
        "gather": gather,
        "slabs": slabs,
        "sums": dict(slabs),
        "relay_sem": pltpu.SemaphoreType.DMA((2, 37)),
        "ring_sem": pltpu.SemaphoreType.DMA((2, RINGS)),
        "load_sem": pltpu.SemaphoreType.DMA((3,)),
    }


def shards(right_side, lower_blocks, upper_blocks, pivot_inverse, widths, first_row):
    vmem = pl.BlockSpec(memory_space=pltpu.VMEM)
    smem = pl.BlockSpec(memory_space=pltpu.SMEM)
    hbm = pl.BlockSpec(memory_space=pl.ANY)
    leaves, tree = jax.tree.flatten(scratch_shapes())

    def body(*refs):
        kernel(*refs[:7], jax.tree.unflatten(tree, refs[7:]))

    return pl.pallas_call(
        body,
        out_shape=jax.ShapeDtypeStruct(right_side.shape, BF),
        in_specs=[vmem, smem, smem, hbm, hbm, hbm],
        out_specs=vmem,
        scratch_shapes=leaves,
        compiler_params=pltpu.CompilerParams(
            collective_id=1, has_side_effects=True, vmem_limit_bytes=56 * 1024 * 1024
        ),
        name="tree_solve",
    )(
        right_side,
        widths,
        first_row.T,
        lower_blocks,
        upper_blocks,
        pivot_inverse,
    )


def solution(mesh):
    in_specs = (
        P(None, ("row", "col"), None),
        P(None, "row", "col"),
        P(None, "row", "col"),
        P(None, "row", "col"),
        P(),
        P(),
    )
    out_specs = P(None, ("row", "col"), None)
    return jax.shard_map(shards, mesh=mesh, in_specs=in_specs, out_specs=out_specs, check_vma=False)
```

```python
import functools

import jax
import jax.numpy as jnp
from jax import lax
from jax.experimental import pallas as pl
from jax.experimental.pallas import tpu as pltpu
from jax.sharding import PartitionSpec as P

MESH = pl.DeviceIdType.MESH
BF = jnp.bfloat16
F32 = jnp.float32
LEVELS = 5
NX, NZ, NC = 4, 8, 8
NQ = NX * NZ
TOP = 2
GROUPS = [1, 1, 1, 2, 4]
GBASE = [7, 7, 6, 4, 0]
NGROUP = 8
GROUP = 16


def block_offsets():
    offsets = {}
    running = 0
    for tree_level in range(1, LEVELS):
        for hop_up in range(tree_level):
            offsets[tree_level, hop_up] = running
            running = running + 2**tree_level
    return offsets


OFF = block_offsets()


def forward_rows(t):
    rows, at = [], 0
    for hop in range(t):
        count = 64 if hop == 0 else 32
        rows.append((t - 1 - hop, at, count))
        at += count
    rows.append((-1, at, 128))
    return rows, at + 128


def backward_rows(t):
    rows, at = [], 0
    for s in range(t + 1, LEVELS):
        count = 32 * (2**s if t == 1 else 4 * 2 ** (s - t))
        rows.append((s, at, count))
        at += count
    return rows, at


FROWS = {t: forward_rows(t) for t in range(TOP, LEVELS)}
BROWS = {t: backward_rows(t) for t in range(1, LEVELS - 1)}
TL, TU, TD, TOPS = 0, 2, 4, 7
R3, R3B, R2, P1, P0, SPLIT, B2, B3, B3B, B4, B4B, PANEL, MPANEL, RINGS = range(14)


def kernel(rs_ref, widths_ref, first_ref, l_hbm, u_hbm, d_hbm, out_ref, scratch):
    row = lax.axis_index("row")
    col = lax.axis_index("col")
    x, z, core = row // 16, (row // 2) % 8, row % 2
    q = x * NZ + z
    other = 1 - core
    lw, uw, dw, sel, perm = (scratch[n] for n in ("lw", "uw", "dw", "sel", "perm"))
    fw, bw, pend, acc = (scratch[n] for n in ("fw", "bw", "pend", "acc"))
    rows_in, rows_out, heap = (scratch[n] for n in ("rows_in", "rows_out", "heap"))
    gather, relay_sem, load_sem = scratch["gather"], scratch["relay_sem"], scratch["load_sem"]
    slabs, sums, ring_sem = scratch["slabs"], scratch["sums"], scratch["ring_sem"]
    panel, mpanel, split = scratch["panel"], scratch["mpanel"], scratch["split"]
    top1, top0, wide_u = scratch["top1"], scratch["top0"], scratch["wide_u"]
    place, packed = scratch["place"], scratch["packed"]

    loads = [
        pltpu.make_async_copy(src, dst, load_sem.at[i])
        for i, (src, dst) in enumerate(((l_hbm, lw), (u_hbm, uw), (d_hbm, dw)))
    ]
    for load in loads:
        load.start()

    barrier = pltpu.get_barrier_semaphore()

    def away(k, n):
        return (n // 2 + (k + 1) // 2 * (1 - 2 * ((k + 1) % 2))) % n

    def plane_peer(k):
        px, pz = (x + away(k // NZ, NX)) % NX, (z + away(k % NZ, NZ)) % NZ
        return (px * NZ + pz) * 2 + core

    def signal(target):
        pl.semaphore_signal(barrier, inc=1, device_id=target, device_id_type=MESH)

    @pl.loop(0, NQ - 1)
    def _(k):
        signal({"row": plane_peer(k)})

    @pl.loop(0, NC - 1)
    def _(k):
        signal({"col": (col + away(k, NC)) % NC})

    signal({"row": q * 2 + other})

    def iota(shape, dim):
        return lax.broadcasted_iota(jnp.int32, shape, dim)

    def table(hit):
        return hit.astype(F32).astype(BF)

    def heap_row(r):
        s = r // 4
        n = jnp.where(s < 16, s + 15, jnp.where(s < 24, s - 9, jnp.where(s < 28, s - 21, s - 28)))
        return n * 4 + r % 4

    heap[124:128] = jnp.zeros((4, 256), F32)
    for n in range(31):
        heap[4 * n : 4 * n + 4] = rs_ref[n].astype(F32)
    order = table(iota((128, 128), 1) == heap_row(iota((128, 128), 0)))
    rows_in[...] = jnp.dot(order, heap[...].astype(BF), preferred_element_type=F32).astype(BF)

    row16 = iota((GROUP, 256), 0)
    own_row = row * 32 + col * 4 + row16 % 4

    def valid(t, g):
        limit = jnp.zeros((GROUP, 256), jnp.int32)
        for j in range(4):
            limit = jnp.where(row16 // 4 == j, widths_ref[2**t - 1 + 4 * g + j], limit)
        return (own_row < limit).astype(F32)

    def piece(t, g):
        at = (GBASE[t] + g) * GROUP
        return slice(at, at + GROUP)

    for g in range(4):
        y = valid(4, g) * rows_in[piece(4, g)].astype(F32)
        gather["f4"][g, core, x, z] = y.astype(BF)

    @pl.loop(0, 2)
    def _(h):
        @pl.loop(0, 8)
        def _(b):
            r = iota((128, 512), 0) + b * 128
            s = iota((128, 512), 1)
            p = (r % 256) // 4
            target = (p // 2) * 16 + (r // 256) * 4 + r % 4
            hit = jnp.logical_and(s == target, p % 2 == h)
            sel[h, pl.ds(pl.multiple_of(b * 128, 128), 128)] = table(hit)

    r, s = iota((128, 128), 0), iota((128, 128), 1)
    perm[...] = table(s == ((r // 4) % 4) * 32 + (r // 16) * 4 + r % 4)

    out_row = row * 32 + iota((32, 256), 0)
    lane = iota((32, 256), 1)
    in_row = (lane // 4) * 32 + col * 4 + lane % 4

    def mask(ref, index, t, hop):
        @pl.loop(0, 2**t)
        def _(n):
            keep = table(index >= first_ref[hop, 2**t - 1 + n])
            ref[OFF[t, hop] + n] = ref[OFF[t, hop] + n] * keep

    def stack(ref, base, groups, members):
        return jnp.concatenate(
            [
                jnp.concatenate([ref[base + 4 * g + j] for j in members], axis=1)
                for g in range(groups)
            ],
            axis=0,
        )

    def expand(left, h, first, last):
        part = sel[h, first * 256 : last * 256]
        return jnp.dot(left, part, preferred_element_type=F32)

    def expand_forward(t, entries):
        groups = GROUPS[t]
        for target, at, count in entries:
            if target >= 0:
                hop = t - 1 - target
                halves = count // 32
                per = 4 // halves
                jobs = [
                    (lw, OFF[t, hop], at + 32 * v, [v * per + w for w in range(per)])
                    for v in range(halves)
                ]
            else:
                jobs = [(dw, 2**t - 1, at + 32 * j, [j]) for j in range(4)]
            for ref, base, first, members in jobs:
                left = stack(ref, base, groups, members)

                @pl.loop(0, 2)
                def _(h):
                    wide = expand(left, h, members[0], members[-1] + 1).astype(BF)
                    for g in range(groups):
                        fw[t][g, h, first : first + 32] = wide[g * 32 : (g + 1) * 32]

    def uppers(s, hop, first, count):
        base = OFF[s, hop] + first
        return uw[base : base + count].reshape(count * 32, 256)

    def expand_backward(t):
        for s, at, count in BROWS[t][0]:
            if t == 1:
                each = 2 ** (s - 1)
                for a in range(2):
                    root = uppers(s, s - 1, a * each, each)
                    parent = uppers(s, s - 2, a * each, each)
                    first = at + a * each * 32

                    @pl.loop(0, 2)
                    def _(h):
                        wide = expand(root, h, 0, 1) + expand(parent, h, 1 + a, 2 + a)
                        bw[t][0, h, first : first + each * 32] = wide.astype(BF)

                continue
            each = 2 ** (s - t)
            for g in range(GROUPS[t]):
                for j in range(4):
                    left = uppers(s, s - 1 - t, (4 * g + j) * each, each)
                    first = at + j * each * 32

                    @pl.loop(0, 2)
                    def _(h):
                        wide = expand(left, h, j, j + 1).astype(BF)
                        bw[t][g, h, first : first + each * 32] = wide

    leaving = []

    def remote(src, dst, number, target):
        return pltpu.make_async_remote_copy(
            src_ref=src,
            dst_ref=dst,
            send_sem=relay_sem.at[0, number],
            recv_sem=relay_sem.at[1, number],
            device_id=target,
            device_id_type=MESH,
        )

    def spread(ref, number):
        @pl.loop(0, NQ - 1)
        def _(k):
            mine = ref.at[core, q]
            remote(mine, mine, number, {"row": plane_peer(k)}).start()

        leaving.append((remote, ref.at[core, 0 : NQ - 1], number, {"row": q * 2 + other}))

    def spread_wait(ref, number):
        some = ref.at[core, 0 : NQ - 1]
        remote(some, some, number, {"row": q * 2 + other}).wait_recv()

    def along_z(mine, some, number):
        @pl.loop(0, NZ - 1)
        def _(k):
            to = (x * NZ + (z + away(k, NZ)) % NZ) * 2 + core
            remote(mine, mine, number, {"row": to}).start()

        leaving.append((remote, some, number, {"row": q * 2 + other}))

    def along_x(mine, some, number):
        @pl.loop(0, NX - 1)
        def _(k):
            to = (((x + away(k, NX)) % NX) * NZ + z) * 2 + core
            remote(mine, mine, number, {"row": to}).start()

        leaving.append((remote, some, number, {"row": q * 2 + other}))

    def landed(some, number):
        remote(some, some, number, {"row": q * 2 + other}).wait_recv()

    def z_first(ref, number):
        along_z(ref.at[core, x, z], ref.at[core, 0, 0 : NZ - 1], number)

    def then_x(ref, number):
        landed(ref.at[core, 0, 0 : NZ - 1], number)
        along_x(ref.at[core, x], ref.at[core, 0 : NX - 1], number + 1)

    def x_landed(ref, number):
        landed(ref.at[core, 0 : NX - 1], number + 1)

    def x_first(ref, number):
        along_x(ref.at[core, x, z], ref.at[core, 0, 0 : NX - 1], number)

    def then_z(ref, number):
        landed(ref.at[core, 0, 0 : NX - 1], number)
        along_z(ref.at[core, :, z], ref.at[core, :, 0 : NZ - 1], number + 1)

    def z_landed(ref, number):
        landed(ref.at[core, :, 0 : NZ - 1], number + 1)

    def share(ref, number):
        half = ref.at[core]
        remote(half, half, number, {"row": q * 2 + other}).start()
        leaving.append((remote, half, number, {"row": q * 2 + other}))

    def share_wait(ref, number):
        half = ref.at[other]
        remote(half, half, number, {"row": q * 2 + other}).wait_recv()

    def ring(src, dst, number, target):
        return pltpu.make_async_remote_copy(
            src_ref=src,
            dst_ref=dst,
            send_sem=ring_sem.at[0, number],
            recv_sem=ring_sem.at[1, number],
            device_id={"col": target},
            device_id_type=MESH,
        )

    def ring_all(landing, number):
        @pl.loop(0, NC - 1)
        def _(k):
            mine = landing.at[col]
            ring(mine, mine, number, (col + away(k, NC)) % NC).start()

        leaving.append((ring, landing.at[0 : NC - 1], number, (col + 1) % NC))

    def ring_wait(landing, number):
        some = landing.at[0 : NC - 1]
        ring(some, some, number, (col + 1) % NC).wait_recv()

    def reduce_start(source, first, groups, number):
        for g in range(groups):
            part = source[(first + g) * 128 : (first + g + 1) * 128].astype(BF)
            cut = jnp.dot(perm[...], part, preferred_element_type=F32).astype(BF)
            slabs[number][:, g * GROUP : (g + 1) * GROUP] = cut.reshape(NC, GROUP, 256)
        reduce_send(number)

    def reduce_send(number):
        slab, landing = slabs[number], sums[number]

        @pl.loop(0, NC - 1)
        def _(k):
            to = (col + away(k, NC)) % NC
            ring(slab.at[to], landing.at[col], number, to).start()

        leaving.append((ring, landing.at[0 : NC - 1], number, (col + 1) % NC))
        landing[col] = slab[col]

    def reduced(number, at):
        landing = sums[number]
        total = landing[0, at].astype(F32)
        for k in range(1, NC):
            total = total + landing[k, at].astype(F32)
        return total

    lane_block = iota((8, 128), 1) // 32

    def pack(blocks):
        total = jnp.where(lane_block == 0, blocks[0], 0.0)
        for b in range(1, 4):
            total = total + jnp.where(lane_block == b, blocks[b], 0.0)
        return total

    def split_start(t, number):
        kind = slabs[number].dtype
        for u in range(2):
            for w in range(4):
                cut = []
                for n in range(2**t):
                    blocks = [
                        pend[t][n * 32 + b * 8 : n * 32 + b * 8 + 8, u * 128 : u * 128 + 128]
                        for b in range(4)
                    ]
                    blocks = [
                        v if b == w else pltpu.roll(v, ((b - w) * 32) % 128, 1)
                        for b, v in enumerate(blocks)
                    ]
                    cut.append(pack(blocks))
                whole = cut[0] if t == 0 else jnp.concatenate(cut, axis=0)
                slabs[number][4 * u + w] = whole.astype(kind)
        reduce_send(number)

    def valid_top(n):
        r = row * 32 + lane_block * 8 + iota((8, 128), 0)
        return (r < widths_ref[n]).astype(F32)

    def fold(wide):
        lanes = iota((32, 128), 1) // 32
        total = jnp.where(lanes == 0, wide[0:32], 0.0)
        for b in range(1, 4):
            total = total + jnp.where(lanes == b, wide[b * 32 : b * 32 + 32], 0.0)
        total = total + pltpu.roll(total, 64, 1)
        total = total + pltpu.roll(total, 32, 1)
        return pack([total[b * 8 : b * 8 + 8] for b in range(4)])

    def top_product(weights, ref, first, count):
        near = ref[core].reshape(NQ * GROUP, 128)
        far = ref[other].reshape(NQ * GROUP, 128)
        rows = slice(first, first + count)
        return jnp.dot(weights[core, rows], near, preferred_element_type=F32) + jnp.dot(
            weights[other, rows], far, preferred_element_type=F32
        )

    def panels(ref, index, b):
        return jnp.concatenate([ref[2 * b, index], ref[2 * b + 1, index]], axis=1)

    def add_forward(t, g, h, ref, entry, start):
        target, at, count = entry
        weights = fw[t][g, h, at : at + count]
        value = jnp.dot(weights, ref[h].reshape(NQ * GROUP, 256), preferred_element_type=F32)
        if target < 0:
            base = g * 128
            if start:
                acc[t][base : base + count] = value
            else:
                acc[t][base : base + count] += value
        else:
            first = ((4 * g) >> (t - target)) * 32
            pend[target][first : first + count] += value

    def add_backward(t, g, h, ref, entry):
        s, at, count = entry
        weights = bw[t][g, h, at : at + count]
        value = jnp.dot(weights, ref[h].reshape(NQ * GROUP, 256), preferred_element_type=F32)
        first = g * 128 * 2 ** (s - t)
        acc[s][first : first + count] -= value

    for load in loads:
        load.wait()
    mask(lw, out_row, 1, 0)
    mask(uw, in_row, 1, 0)
    for n in range(2):
        panel[col, TL + n] = lw[OFF[1, 0] + n]
        panel[col, TU + n] = uw[OFF[1, 0] + n]
    d0 = gather["d0"]
    inside = dw[0] * table(out_row < widths_ref[0])
    panel[col, TD] = inside
    d0[core, x, z] = inside
    for n in range(1, 3):
        panel[col, TD + n] = dw[n]
    pl.semaphore_wait(barrier, NQ - 1 + NC - 1 + 1)

    f4, f3, b3 = gather["f4"], gather["f3"], gather["b3"]
    x_first(f4.at[3], 9)
    for g in range(3):
        z_first(f4.at[g], 3 * g)
    ring_all(panel, PANEL)

    e, f = iota((96, GROUP), 0), iota((96, GROUP), 1)
    expanded = table(jnp.logical_and(e // 32 == f // 4, e % 32 == col * 4 + f % 4))
    begun = -jnp.dot(expanded, rows_in[piece(0, 0)], preferred_element_type=F32)
    pend[0][...] = begun[0:32]
    pend[1][...] = begun[32:96]
    for t in range(2, 4):
        pend[t][...] = jnp.zeros_like(pend[t])
    mask(lw, out_row, 4, 0)
    expand_forward(4, FROWS[4][0][:1])
    then_z(f4.at[3], 9)
    for t in range(4, 1, -1):
        for hop in range(t):
            if (t, hop) != (4, 0):
                mask(lw, out_row, t, hop)
    then_x(f4.at[0], 0)
    expand_forward(4, FROWS[4][0][1:3])
    then_x(f4.at[1], 3)
    then_x(f4.at[2], 6)
    z_first(d0, 12)
    expand_forward(4, FROWS[4][0][3:])
    parents = FROWS[4][0][0]
    for g in range(4):
        (x_landed if g < 3 else z_landed)(f4.at[g], 3 * g)
        share(f4.at[g], 3 * g + 2)
        if g > 0:
            add_forward(4, g - 1, core, f4.at[g - 1], parents, True)
    for g in range(4):
        share_wait(f4.at[g], 3 * g + 2)
        add_forward(4, g, other, f4.at[g], parents, False)
        if g == 1:
            reduce_start(pend[3], 0, 1, R3)
            add_forward(4, 3, core, f4.at[3], parents, True)
    reduce_start(pend[3], 1, 1, R3B)
    then_x(d0, 12)
    for g in range(4):
        for entry in FROWS[4][0][1:]:
            add_forward(4, g, core, f4.at[g], entry, True)
            add_forward(4, g, other, f4.at[g], entry, False)

    expand_forward(3, FROWS[3][0])

    for g, number in enumerate((R3, R3B)):
        ring_wait(sums[number], number)
        y = rows_in[piece(3, g)].astype(F32) - reduced(number, slice(0, GROUP))
        f3[g, core, x, z] = (valid(3, g) * y).astype(BF)
        if g == 0:
            z_first(f3.at[0], 14)
    x_first(f3.at[1], 17)
    then_z(f3.at[1], 17)
    ring_wait(panel, PANEL)
    left = jnp.concatenate(
        [
            jnp.concatenate([panels(panel, TL, b), panels(panel, TL + 1, b)], axis=1)
            for b in range(4)
        ],
        axis=0,
    )

    @pl.loop(0, 2)
    def _(h):
        top1[h, 0:128] = expand(left, h, 0, 4).astype(BF)

    then_x(f3.at[0], 14)
    x_landed(d0, 12)
    share(d0, 32)
    for g in range(2):
        left = jnp.concatenate(
            [
                jnp.concatenate([panel[4 * g + j, TU + n] for j in range(4)], axis=1)
                for n in range(2)
            ],
            axis=0,
        )

        @pl.loop(0, 2)
        def _(h):
            wide_u[g, h] = expand(left, h, 0, 4).astype(BF)

    for n in range(3):
        left = jnp.concatenate([panels(panel, TD + n, b) for b in range(4)], axis=0)

        @pl.loop(0, 2)
        def _(h):
            if n == 0:
                top0[h, 0:128] = expand(left, h, 0, 2).astype(BF)
            else:
                wide = expand(left, h, 2 * n - 2, 2 * n).astype(BF)
                top1[h, n * 128 : n * 128 + 128] = wide

    parents = FROWS[3][0][0]
    x_landed(f3.at[0], 14)
    share(f3.at[0], 16)
    add_forward(3, 0, core, f3.at[0], parents, True)
    z_landed(f3.at[1], 17)
    share(f3.at[1], 19)
    share_wait(f3.at[0], 16)
    add_forward(3, 0, other, f3.at[0], parents, False)
    add_forward(3, 1, core, f3.at[1], parents, True)
    share_wait(f3.at[1], 19)
    add_forward(3, 1, other, f3.at[1], parents, False)
    reduce_start(pend[2], 0, 1, R2)
    for g in range(2):
        for entry in FROWS[3][0][1:]:
            add_forward(3, g, core, f3.at[g], entry, True)
            add_forward(3, g, other, f3.at[g], entry, False)
    expand_forward(2, FROWS[2][0])
    share_wait(d0, 32)
    product = jnp.zeros((64, 256), F32)
    for g in range(2):
        for h in range(2):
            block = d0[h, :, :, g * GROUP : (g + 1) * GROUP].reshape(NQ * GROUP, 256)
            product = product + jnp.dot(wide_u[g, h], block, preferred_element_type=F32)
    mpanel[col] = product.astype(BF).reshape(2, 32, 256)

    ref = gather["f2"]
    ring_wait(sums[R2], R2)
    y = rows_in[piece(2, 0)].astype(F32) - reduced(R2, slice(0, GROUP))
    ref[core, q] = (valid(2, 0) * y).astype(BF)
    spread(ref, 20)
    ring_all(mpanel, MPANEL)
    for s in range(2, LEVELS):
        for hop in range(s):
            mask(uw, in_row, s, hop)
    expand_backward(1)
    spread_wait(ref, 20)
    share(ref, 21)
    parents = FROWS[2][0][0]
    add_forward(2, 0, core, ref, parents, True)
    share_wait(ref, 21)
    add_forward(2, 0, other, ref, parents, False)
    split_start(1, P1)
    for entry in FROWS[2][0][1:]:
        add_forward(2, 0, core, ref, entry, True)
        add_forward(2, 0, other, ref, entry, False)

    split_start(0, P0)
    @pl.loop(0, 8)
    def _(b):
        r, s = iota((128, 256), 0), iota((128, 256), 1)
        hit = jnp.logical_and(r // 32 == col // 2, s == b * 32 + r % 32)
        place[pl.ds(pl.multiple_of(b * 128, 128), 128)] = table(hit)

    y1 = gather["y1"]
    ring_wait(sums[P1], P1)
    solved = -reduced(P1, slice(0, GROUP))
    for n in range(2):
        packed[n * 8 : n * 8 + 8] = valid_top(1 + n) * solved[n * 8 : n * 8 + 8]
    y1[core, q] = packed[...].astype(BF)
    spread(y1, 22)
    expand_backward(2)
    ring_wait(sums[P0], P0)
    spread_wait(y1, 22)
    share(y1, 23)
    share_wait(y1, 23)
    y0 = -reduced(P0, slice(0, 8)) - fold(top_product(top1, y1, 0, 128))
    y0 = valid_top(0) * y0
    ref = gather["y0"]
    packed[0:8] = y0
    packed[8:16] = jnp.zeros((8, 128), F32)
    ref[core, q] = packed[...].astype(BF)
    spread(ref, 24)
    wide = top_product(top1, y1, 128, 256)
    scaled = [fold(wide[n * 128 : n * 128 + 128]) for n in range(2)]
    ring_wait(mpanel, MPANEL)
    for n in range(2):
        left = jnp.concatenate([panels(mpanel, n, b) for b in range(4)], axis=0)

        @pl.loop(0, 2)
        def _(h):
            wide = expand(left, h, 0, 2).astype(BF)
            top0[h, 128 + n * 128 : 256 + n * 128] = wide

    expand_backward(3)
    spread_wait(ref, 24)
    share(ref, 25)
    share_wait(ref, 25)
    wide = top_product(top0, ref, 0, 384)
    split[col, 0:8] = (valid_top(0) * fold(wide[0:128])).astype(BF)
    for n in range(2):
        s1 = scaled[n] - fold(wide[128 + n * 128 : 256 + n * 128])
        packed[n * 8 : n * 8 + 8] = valid_top(1 + n) * s1
    split[col, 8:24] = packed[...].astype(BF)
    split[col, 24:32] = jnp.zeros((8, 128), BF)
    ring_all(split, SPLIT)
    e, f = iota((GROUP, 32), 0), iota((GROUP, 32), 1)
    rows = table(f == (e // 4) * 8 + (col % 2) * 4 + e % 4)
    ring_wait(split, SPLIT)
    side = jnp.concatenate([split[k] for k in range(NC)], axis=1)
    side = jnp.dot(side, place[...], preferred_element_type=F32).astype(BF)
    solved = jnp.dot(rows, side, preferred_element_type=F32).astype(BF)
    rows_out[piece(0, 0)] = solved

    gather["b1"][core, q] = solved
    for t, number, ringed in ((1, 26, None), (2, 28, B2)):
        ref = gather[f"b{t}"]
        if t == 2:
            ring_wait(sums[B2], B2)
            solved = (valid(2, 0) * reduced(B2, slice(0, GROUP))).astype(BF)
            rows_out[piece(2, 0)] = solved
            ref[core, q] = solved
        spread(ref, number)
        spread_wait(ref, number)
        share(ref, number + 1)
        children = BROWS[t][0][0]
        add_backward(t, 0, core, ref, children)
        share_wait(ref, number + 1)
        add_backward(t, 0, other, ref, children)
        reduce_start(acc[t + 1], 0, 1, {1: B2, 2: B3}[t])
        if t == 2:
            reduce_start(acc[3], 1, 1, B3B)
        for entry in BROWS[t][0][1:]:
            add_backward(t, 0, core, ref, entry)
            add_backward(t, 0, other, ref, entry)
    for g, number in enumerate((B3, B3B)):
        ring_wait(sums[number], number)
        solved = (valid(3, g) * reduced(number, slice(0, GROUP))).astype(BF)
        rows_out[piece(3, g)] = solved
        b3[g, core, x, z] = solved
        if g == 0:
            z_first(b3.at[0], 30)
    x_first(b3.at[1], 33)
    then_z(b3.at[1], 33)
    then_x(b3.at[0], 30)
    children = BROWS[3][0][0]
    x_landed(b3.at[0], 30)
    share(b3.at[0], 35)
    add_backward(3, 0, core, b3.at[0], children)
    z_landed(b3.at[1], 33)
    share(b3.at[1], 36)
    share_wait(b3.at[0], 35)
    add_backward(3, 0, other, b3.at[0], children)
    reduce_start(acc[4], 0, 2, B4)
    add_backward(3, 1, core, b3.at[1], children)
    share_wait(b3.at[1], 36)
    add_backward(3, 1, other, b3.at[1], children)
    reduce_start(acc[4], 2, 2, B4B)
    for g in range(4):
        number = (B4, B4B)[g // 2]
        if g % 2 == 0:
            ring_wait(sums[number], number)
        at = slice(g % 2 * GROUP, (g % 2 + 1) * GROUP)
        rows_out[piece(4, g)] = (valid(4, g) * reduced(number, at)).astype(BF)

    order = table(iota((128, 128), 0) == heap_row(iota((128, 128), 1)))
    heap[...] = jnp.dot(order, rows_out[...], preferred_element_type=F32)
    for n in range(31):
        out_ref[n] = heap[4 * n : 4 * n + 4].astype(BF)

    for kind, ref, number, target in leaving:
        kind(ref, ref, number, target).wait_send()


def scratch_shapes():
    gather = {
        "f4": pltpu.VMEM((4, 2, NX, NZ, GROUP, 256), BF),
        "f3": pltpu.VMEM((2, 2, NX, NZ, GROUP, 256), BF),
        "b3": pltpu.VMEM((2, 2, NX, NZ, GROUP, 256), BF),
        "d0": pltpu.VMEM((2, NX, NZ, 2 * GROUP, 256), BF),
        "y1": pltpu.VMEM((2, NQ, GROUP, 128), BF),
        "y0": pltpu.VMEM((2, NQ, GROUP, 128), BF),
    }
    for name in ("f2", "b1", "b2"):
        gather[name] = pltpu.VMEM((2, NQ, GROUP, 256), BF)
    slabs = {n: pltpu.VMEM((NC, GROUP, 256), BF) for n in (R3, R3B, R2, B2, B3, B3B)}
    slabs |= {n: pltpu.VMEM((NC, 2 * GROUP, 256), BF) for n in (B4, B4B)}
    slabs[P1] = pltpu.VMEM((NC, GROUP, 128), BF)
    slabs[P0] = pltpu.VMEM((NC, 8, 128), F32)
    return {
        "lw": pltpu.VMEM((98, 32, 256), BF),
        "uw": pltpu.VMEM((98, 32, 256), BF),
        "dw": pltpu.VMEM((31, 32, 256), BF),
        "rows_in": pltpu.VMEM((128, 256), BF),
        "rows_out": pltpu.VMEM((128, 256), BF),
        "heap": pltpu.VMEM((128, 256), F32),
        "sel": pltpu.VMEM((2, 1024, 512), BF),
        "perm": pltpu.VMEM((128, 128), BF),
        "place": pltpu.VMEM((1024, 256), BF),
        "packed": pltpu.VMEM((GROUP, 128), F32),
        "fw": {t: pltpu.VMEM((GROUPS[t], 2, FROWS[t][1], 512), BF) for t in FROWS},
        "bw": {t: pltpu.VMEM((GROUPS[t], 2, BROWS[t][1], 512), BF) for t in BROWS},
        "top1": pltpu.VMEM((2, 384, 512), BF),
        "top0": pltpu.VMEM((2, 384, 512), BF),
        "wide_u": pltpu.VMEM((2, 2, 64, 512), BF),
        "panel": pltpu.VMEM((NC, TOPS, 32, 256), BF),
        "mpanel": pltpu.VMEM((NC, 2, 32, 256), BF),
        "split": pltpu.VMEM((NC, 32, 128), BF),
        "pend": [pltpu.VMEM((32 * 2**t, 256), F32) for t in range(4)],
        "acc": {t: pltpu.VMEM((32 * 2**t, 256), F32) for t in range(TOP, LEVELS)},
        "gather": gather,
        "slabs": slabs,
        "sums": dict(slabs),
        "relay_sem": pltpu.SemaphoreType.DMA((2, 37)),
        "ring_sem": pltpu.SemaphoreType.DMA((2, RINGS)),
        "load_sem": pltpu.SemaphoreType.DMA((3,)),
    }


def shards(right_side, lower_blocks, upper_blocks, pivot_inverse, widths, first_row):
    vmem = pl.BlockSpec(memory_space=pltpu.VMEM)
    smem = pl.BlockSpec(memory_space=pltpu.SMEM)
    hbm = pl.BlockSpec(memory_space=pl.ANY)
    leaves, tree = jax.tree.flatten(scratch_shapes())

    def body(*refs):
        kernel(*refs[:7], jax.tree.unflatten(tree, refs[7:]))

    return pl.pallas_call(
        body,
        out_shape=jax.ShapeDtypeStruct(right_side.shape, BF),
        in_specs=[vmem, smem, smem, hbm, hbm, hbm],
        out_specs=vmem,
        scratch_shapes=leaves,
        compiler_params=pltpu.CompilerParams(
            collective_id=1, has_side_effects=True, vmem_limit_bytes=56 * 1024 * 1024
        ),
        name="tree_solve",
    )(
        right_side,
        widths,
        first_row.T,
        lower_blocks,
        upper_blocks,
        pivot_inverse,
    )


def solution(mesh):
    in_specs = (
        P(None, ("row", "col"), None),
        P(None, "row", "col"),
        P(None, "row", "col"),
        P(None, "row", "col"),
        P(),
        P(),
    )
    out_specs = P(None, ("row", "col"), None)
    return jax.shard_map(shards, mesh=mesh, in_specs=in_specs, out_specs=out_specs, check_vma=False)
```
